256 devices in a mesh: dp: 16 (over z_lo, y), expert: 16 (over x, z_hi, core).
Axes of the slice: x: 4, y: 4, z: 8 (z_hi: 2, z_lo: 4; z = z_hi * 4 + z_lo), core: 2. Of those that a mesh axis runs over, the one named last changes fastest.
Arguments:
- tokens: bfloat16 [512, 256, 1280], P(('dp', 'expert')), may hold values from -10 to 10, as said below
- slot_keys: bfloat16 [1280, 32], replicated, may hold values from -2 to 2
- w_in: bfloat16 [32, 1280, 5120], P('expert', None, 'dp'), may hold values from -0.15625 to 0.15625
- w_out: bfloat16 [32, 5120, 1280], P('expert', 'dp'), may hold values from -0.078125 to 0.078125
- grad_out: bfloat16 [512, 256, 1280], P(('dp', 'expert')), may hold values from -6 to 6
Outputs:
- grad_tokens: bfloat16 [512, 256, 1280], P(('dp', 'expert'))
- grad_keys: float32 [1280, 32], replicated
- grad_w_in: bfloat16 [32, 1280, 5120], P('expert', None, 'dp')
- grad_w_out: bfloat16 [32, 5120, 1280], P('expert', 'dp')
The draws below stay inside these ranges and needn't reach their ends.
Inputs may be any that keep to these rules, and one draw needn't show every extreme that they name: `tokens`: patch features of order one.
All inputs are finite; a program needn't handle non-finite values.
Results may differ from the reference program's by a relative error of at most 0.029.
Values may be sent and summed in bfloat16 or wider, within the bound.
A program may use at most 128 MiB of HBM per device.

```python
import math
import jax
import jax.numpy as jnp
from jax import lax

D = 1280
F = 5120
P_SIZE = 256
IMAGES = 512
EXPERTS = 32


def base_columns(key):
    return jnp.clip(jax.random.normal(key, (D, EXPERTS), jnp.float32), -4.0, 4.0)


def draw_slot_keys(key, part):
    columns = base_columns(key)
    return (columns * (3.0 / math.sqrt(D))).astype(jnp.bfloat16)


def draw_tokens(key, part):
    key = jax.random.fold_in(key, 23)
    key_drawn = jax.random.fold_in(key, 1)
    values = jnp.clip(jax.random.normal(key_drawn, (IMAGES, P_SIZE, D), jnp.float32), -6.0, 6.0)
    return jnp.clip(values, -10.0, 10.0).astype(jnp.bfloat16)


def level_of(stream_key, shape, shards, smallest, largest):
    def one(dim, shards_of):
        draws = jax.random.uniform(jax.random.fold_in(jax.random.fold_in(stream_key, 6), dim), (shards_of,), jnp.float32, smallest / len(shards), largest / len(shards))
        return jnp.repeat(jnp.exp(draws), shape[dim] // shards_of).reshape((-1,) + (1,) * (len(shape) - dim - 1))

    level = one(*shards[0])
    for cut in shards[1:]:
        level = level * one(*cut)
    return level


def noise(key, dims, width, most, cuts=(), kind=jnp.bfloat16):
    values = jax.random.normal(key, dims, jnp.float32) * width
    if len(cuts) > 0:
        values = level_of(key, dims, cuts, -0.22, 0.18) * values
    return jnp.clip(values, min=-most, max=most).astype(kind)


def setup_inputs(seed: int = 0) -> dict:
    key_list = jax.random.split(jax.random.key(seed), 6)
    return {
        "tokens": draw_tokens(jax.random.fold_in(key_list[5], 71), 0),
        "slot_keys": draw_slot_keys(jax.random.fold_in(key_list[5], 71), 0),
        "w_in": noise(key_list[2], (EXPERTS, D, F), D ** -0.5, 0.15625, ((0, 16), (2, 16))),
        "w_out": noise(key_list[3], (EXPERTS, F, D), F ** -0.5, 0.078125, ((0, 16), (1, 16))),
        "grad_out": noise(key_list[4], (IMAGES, P_SIZE, D), 1.0, 6.0, ((0, 256),)),
    }


INV_ROOT2 = 0.7071067811865476
INV_ROOT_TWO_PI = 0.3989422804014327


def gelu_value(pre_act):
    return 0.5 * pre_act * (1.0 + jax.scipy.special.erf(pre_act * INV_ROOT2))


def gelu_slope(pre_act):
    return 0.5 * (1.0 + jax.scipy.special.erf(pre_act * INV_ROOT2)) + pre_act * jnp.exp(-0.5 * pre_act * pre_act) * INV_ROOT_TWO_PI


def expert_pass(operands):
    slot_rows, grad_rows, first_proj, second_proj = operands
    pre_act = jnp.dot(slot_rows, first_proj, preferred_element_type=jnp.float32)
    hidden_act = gelu_value(pre_act).astype(jnp.bfloat16)
    act_grad = jnp.dot(grad_rows, second_proj.T, preferred_element_type=jnp.float32)
    pre_grad = (act_grad * gelu_slope(pre_act)).astype(jnp.bfloat16)
    out_rows = jnp.dot(hidden_act, second_proj, preferred_element_type=jnp.float32).astype(jnp.bfloat16)
    back_rows = jnp.dot(pre_grad, first_proj.T, preferred_element_type=jnp.float32).astype(jnp.bfloat16)
    grad_first = jnp.dot(slot_rows.T, pre_grad, preferred_element_type=jnp.float32).astype(jnp.bfloat16)
    grad_second = jnp.dot(hidden_act.T, grad_rows, preferred_element_type=jnp.float32).astype(jnp.bfloat16)
    return out_rows, back_rows, grad_first, grad_second


def reference(tokens, slot_keys, w_in, w_out, grad_out):
    tok_wide = tokens.astype(jnp.float32)
    grad_wide = grad_out.astype(jnp.float32)
    keys_wide = slot_keys.astype(jnp.float32)
    logits = jnp.einsum("bpd,ds->bps", tok_wide, keys_wide)
    dispatch = jax.nn.softmax(logits, axis=1)
    combine = jax.nn.softmax(logits, axis=2)
    dispatch_low = dispatch.astype(jnp.bfloat16)
    combine_low = combine.astype(jnp.bfloat16)
    slot_in = jnp.einsum("bps,bpd->bsd", dispatch_low.astype(jnp.float32), tok_wide).astype(jnp.bfloat16)
    slot_grad = jnp.einsum("bps,bpd->bsd", combine_low.astype(jnp.float32), grad_wide).astype(jnp.bfloat16)
    out_rows, back_rows, grad_w_in, grad_w_out = lax.map(
        expert_pass, (slot_in.transpose(1, 0, 2), slot_grad.transpose(1, 0, 2), w_in, w_out))
    slot_out = out_rows.transpose(1, 0, 2).astype(jnp.float32)
    slot_dx = back_rows.transpose(1, 0, 2).astype(jnp.float32)
    comb_grad = jnp.einsum("bpd,bsd->bps", grad_wide, slot_out)
    comb_logit = combine * (comb_grad - jnp.sum(combine * comb_grad, axis=2, keepdims=True))
    disp_grad = jnp.einsum("bpd,bsd->bps", tok_wide, slot_dx)
    disp_logit = dispatch * (disp_grad - jnp.sum(dispatch * disp_grad, axis=1, keepdims=True))
    logit_grad = (comb_logit + disp_logit).astype(jnp.bfloat16).astype(jnp.float32)
    grad_tokens = (jnp.einsum("bps,bsd->bpd", dispatch_low.astype(jnp.float32), slot_dx)
                   + jnp.einsum("bps,ds->bpd", logit_grad, keys_wide)).astype(jnp.bfloat16)
    grad_keys = jnp.einsum("bpd,bps->ds", tok_wide, logit_grad)
    return grad_tokens, grad_keys, grad_w_in, grad_w_out
```

```python
import jax
import jax.numpy as jnp
from jax import lax
from jax.experimental import pallas as pl
from jax.experimental.pallas import tpu as pltpu
from jax.sharding import PartitionSpec as P

MESH = pl.DeviceIdType.MESH
GROUP = 16

INV_ROOT2 = 0.7071067811865476
INV_ROOT_TWO_PI = 0.3989422804014327


def gelu_value(pre_act):
    return 0.5 * pre_act * (1.0 + jax.scipy.special.erf(pre_act * INV_ROOT2))


def gelu_slope(pre_act):
    return (
        0.5 * (1.0 + jax.scipy.special.erf(pre_act * INV_ROOT2))
        + pre_act * jnp.exp(-0.5 * pre_act * pre_act) * INV_ROOT_TWO_PI
    )


def sum_kernel(x_ref, out_ref, src, landed_a, landed_b, part, total, send, recv):
    row, col = lax.axis_index("dp"), lax.axis_index("expert")

    def at(axis, offset):
        if axis == 0:
            return (lax.rem(row + offset, GROUP), col)
        return (row, lax.rem(col + offset, GROUP))

    barrier = pltpu.get_barrier_semaphore()

    @pl.loop(1, GROUP)
    def _(o):
        for axis in range(2):
            pl.semaphore_signal(barrier, inc=1, device_id=at(axis, o), device_id_type=MESH)

    tiles = x_ref.shape[0]
    src[pl.ds(0, tiles)] = x_ref[...]
    src[pl.ds(tiles, src.shape[0] - tiles)] = jnp.zeros(
        (src.shape[0] - tiles,) + src.shape[1:], src.dtype
    )
    pl.semaphore_wait(barrier, 2 * (GROUP - 1))

    def copy(round_, o):
        if round_ == 0:
            there = at(0, o)
            a, b = src.at[pl.ds(3 * there[0], 3)], landed_a.at[o]
        elif round_ == 1:
            there = at(1, o)
            a, b = part, landed_b.at[o]
        else:
            there = at(0, o)
            a, b = total, out_ref.at[row]
        return pltpu.make_async_remote_copy(
            src_ref=a,
            dst_ref=b,
            send_sem=send.at[round_, o],
            recv_sem=recv.at[round_, o],
            device_id=there,
            device_id_type=MESH,
        )

    def start(round_):
        @pl.loop(1, GROUP)
        def _(o):
            copy(round_, o).start()

    def finish(round_):
        @pl.loop(1, GROUP)
        def _(o):
            copy(round_, o).wait_recv()

    start(0)
    finish(0)
    acc = src[pl.ds(3 * row, 3)]
    for o in range(1, GROUP):
        acc = acc + landed_a[o]
    part[...] = acc
    start(1)
    finish(1)
    acc = jnp.zeros(part.shape, part.dtype)
    landed_b[0] = part[...]
    for c in range(GROUP):
        acc = acc + landed_b[lax.rem(col - c + GROUP, GROUP)]
    total[...] = acc
    start(2)
    out_ref[row] = acc
    finish(2)

    @pl.loop(1, GROUP)
    def _(o):
        for r in range(3):
            copy(r, o).wait_send()


def sum_over_devices(x):
    chunk = (3, 8, 128)
    out = pl.pallas_call(
        sum_kernel,
        out_shape=jax.ShapeDtypeStruct((GROUP,) + chunk, jnp.float32),
        in_specs=[pl.BlockSpec(memory_space=pltpu.VMEM)],
        out_specs=pl.BlockSpec(memory_space=pltpu.VMEM),
        scratch_shapes=[
            pltpu.VMEM((3 * GROUP, 8, 128), jnp.float32),
            pltpu.VMEM((GROUP,) + chunk, jnp.float32),
            pltpu.VMEM((GROUP,) + chunk, jnp.float32),
            pltpu.VMEM(chunk, jnp.float32),
            pltpu.VMEM(chunk, jnp.float32),
            pltpu.SemaphoreType.DMA((3, GROUP)),
            pltpu.SemaphoreType.DMA((3, GROUP)),
        ],
        compiler_params=pltpu.CompilerParams(collective_id=1, has_side_effects=True),
        name="sum_keys",
    )(x)
    return out.reshape(3 * GROUP, 8, 128)[: x.shape[0]]


def local(tokens, slot_keys, w_in, w_out, grad_out):
    logits = jnp.einsum("bpd,ds->bps", tokens, slot_keys, preferred_element_type=jnp.float32)
    dispatch = jax.nn.softmax(logits, axis=1)
    combine = jax.nn.softmax(logits, axis=2)
    dispatch_low = dispatch.astype(jnp.bfloat16)
    combine_low = combine.astype(jnp.bfloat16)
    slot_in = jnp.einsum(
        "bps,bpd->bsd", dispatch_low, tokens, preferred_element_type=jnp.float32
    ).astype(jnp.bfloat16)
    slot_grad = jnp.einsum(
        "bps,bpd->bsd", combine_low, grad_out, preferred_element_type=jnp.float32
    ).astype(jnp.bfloat16)
    sent_in, sent_grad = (
        lax.all_to_all(slot_in, "expert", split_axis=1, concat_axis=0, tiled=True),
        lax.all_to_all(slot_grad, "expert", split_axis=1, concat_axis=0, tiled=True),
    )
    rows_in, rows_grad = (
        lax.all_gather(sent_in, "dp", axis=0, tiled=True),
        lax.all_gather(sent_grad, "dp", axis=0, tiled=True),
    )
    pre_act = jnp.einsum("rkd,kdf->rkf", rows_in, w_in, preferred_element_type=jnp.float32)
    hidden_act = gelu_value(pre_act).astype(jnp.bfloat16)
    act_grad = jnp.einsum("rkd,kfd->rkf", rows_grad, w_out, preferred_element_type=jnp.float32)
    pre_grad = (act_grad * gelu_slope(pre_act)).astype(jnp.bfloat16)
    grad_w_out = jnp.einsum(
        "rkf,rkd->kfd", hidden_act, rows_grad, preferred_element_type=jnp.float32
    ).astype(jnp.bfloat16)
    grad_w_in = jnp.einsum(
        "rkd,rkf->kdf", rows_in, pre_grad, preferred_element_type=jnp.float32
    ).astype(jnp.bfloat16)
    summed_out = lax.psum_scatter(
        jnp.einsum("rkf,kfd->rkd", hidden_act, w_out, preferred_element_type=jnp.float32).astype(
            jnp.bfloat16
        ),
        "dp",
        scatter_dimension=0,
        tiled=True,
    )
    slot_out = lax.all_to_all(summed_out, "expert", split_axis=0, concat_axis=1, tiled=True)
    summed_dx = lax.psum_scatter(
        jnp.einsum("rkf,kdf->rkd", pre_grad, w_in, preferred_element_type=jnp.float32).astype(
            jnp.bfloat16
        ),
        "dp",
        scatter_dimension=0,
        tiled=True,
    )
    slot_dx = lax.all_to_all(summed_dx, "expert", split_axis=0, concat_axis=1, tiled=True)
    comb_grad = jnp.einsum("bpd,bsd->bps", grad_out, slot_out, preferred_element_type=jnp.float32)
    comb_logit = combine * (comb_grad - jnp.sum(combine * comb_grad, axis=2, keepdims=True))
    disp_grad = jnp.einsum("bpd,bsd->bps", tokens, slot_dx, preferred_element_type=jnp.float32)
    disp_logit = dispatch * (disp_grad - jnp.sum(dispatch * disp_grad, axis=1, keepdims=True))
    logit_grad = (comb_logit + disp_logit).astype(jnp.bfloat16)
    grad_tokens = (
        jnp.einsum("bps,bsd->bpd", dispatch_low, slot_dx, preferred_element_type=jnp.float32)
        + jnp.einsum("bps,ds->bpd", logit_grad, slot_keys, preferred_element_type=jnp.float32)
    ).astype(jnp.bfloat16)
    key_terms = jnp.einsum("bpd,bps->sd", tokens, logit_grad, preferred_element_type=jnp.float32)
    slots, width = key_terms.shape
    tiles = key_terms.reshape(slots // 8, 8, width // 128, 128).transpose(0, 2, 1, 3)
    summed = sum_over_devices(tiles.reshape(-1, 8, 128))
    summed = summed.reshape(slots // 8, width // 128, 8, 128).transpose(0, 2, 1, 3)
    grad_keys = summed.reshape(slots, width).T
    return (grad_tokens, grad_keys, grad_w_in, grad_w_out)


def solution(mesh):
    return jax.shard_map(
        local,
        mesh=mesh,
        in_specs=(
            P(("dp", "expert"), None, None),
            P(),
            P("expert", None, "dp"),
            P("expert", "dp", None),
            P(("dp", "expert"), None, None),
        ),
        out_specs=(
            P(("dp", "expert"), None, None),
            P(),
            P("expert", None, "dp"),
            P("expert", "dp", None),
        ),
        check_vma=False,
    )
```

```python
import jax
import jax.numpy as jnp
from jax import lax
from jax.experimental import pallas as pl
from jax.experimental.pallas import tpu as pltpu
from jax.sharding import PartitionSpec as P

MESH = pl.DeviceIdType.MESH
GROUP = 16
Z, Y = 4, 4
D = 1280
HID = 320
HALF = D // 2
PIECE = 16

INV_ROOT2 = 0.7071067811865476
INV_ROOT_TWO_PI = 0.3989422804014327


def sum_kernel(x_ref, out_ref, src, landed_a, landed_b, part, total, send, recv):
    row, col = lax.axis_index("dp"), lax.axis_index("expert")

    def at(axis, offset):
        if axis == 0:
            return (lax.rem(row + offset, GROUP), col)
        return (row, lax.rem(col + offset, GROUP))

    barrier = pltpu.get_barrier_semaphore()

    @pl.loop(1, GROUP)
    def _(o):
        for axis in range(2):
            pl.semaphore_signal(barrier, inc=1, device_id=at(axis, o), device_id_type=MESH)

    tiles = x_ref.shape[0]
    src[pl.ds(0, tiles)] = x_ref[...]
    src[pl.ds(tiles, src.shape[0] - tiles)] = jnp.zeros(
        (src.shape[0] - tiles,) + src.shape[1:], src.dtype
    )
    pl.semaphore_wait(barrier, 2 * (GROUP - 1))

    def copy(round_, o):
        if round_ == 0:
            there = at(0, o)
            a, b = src.at[pl.ds(3 * there[0], 3)], landed_a.at[o]
        elif round_ == 1:
            there = at(1, o)
            a, b = part, landed_b.at[o]
        else:
            there = at(0, o)
            a, b = total, out_ref.at[row]
        return pltpu.make_async_remote_copy(
            src_ref=a,
            dst_ref=b,
            send_sem=send.at[round_, o],
            recv_sem=recv.at[round_, o],
            device_id=there,
            device_id_type=MESH,
        )

    def start(round_):
        @pl.loop(1, GROUP)
        def _(o):
            copy(round_, o).start()

    def finish(round_):
        @pl.loop(1, GROUP)
        def _(o):
            copy(round_, o).wait_recv()

    start(0)
    finish(0)
    acc = src[pl.ds(3 * row, 3)]
    for o in range(1, GROUP):
        acc = acc + landed_a[o]
    part[...] = acc
    start(1)
    finish(1)
    acc = jnp.zeros(part.shape, part.dtype)
    landed_b[0] = part[...]
    for c in range(GROUP):
        acc = acc + landed_b[lax.rem(col - c + GROUP, GROUP)]
    total[...] = acc
    start(2)
    out_ref[row] = acc
    finish(2)

    @pl.loop(1, GROUP)
    def _(o):
        for r in range(3):
            copy(r, o).wait_send()


def sum_over_devices(x):
    chunk = (3, 8, 128)
    out = pl.pallas_call(
        sum_kernel,
        out_shape=jax.ShapeDtypeStruct((GROUP,) + chunk, jnp.float32),
        in_specs=[pl.BlockSpec(memory_space=pltpu.VMEM)],
        out_specs=pl.BlockSpec(memory_space=pltpu.VMEM),
        scratch_shapes=[
            pltpu.VMEM((3 * GROUP, 8, 128), jnp.float32),
            pltpu.VMEM((GROUP,) + chunk, jnp.float32),
            pltpu.VMEM((GROUP,) + chunk, jnp.float32),
            pltpu.VMEM(chunk, jnp.float32),
            pltpu.VMEM(chunk, jnp.float32),
            pltpu.SemaphoreType.DMA((3, GROUP)),
            pltpu.SemaphoreType.DMA((3, GROUP)),
        ],
        compiler_params=pltpu.CompilerParams(collective_id=1, has_side_effects=True),
        name="sum_keys",
    )(x)
    return out.reshape(3 * GROUP, 8, 128)[: x.shape[0]]


def exchange_kernel(
    pieces_ref, w_in_ref, w_out_ref,
    back_ref, grad_in_ref, grad_out_ref,
    landed, rows, part, hid, pre, from_left, from_right, sum_left, sum_right, sum_z,
    ready, send_x, recv_x, send_b, recv_b, send_z, recv_z, send_y, recv_y, send_h, recv_h,
    send_p, recv_p, send_f, recv_f, send_s, recv_s,
):
    row, col = lax.axis_index("dp"), lax.axis_index("expert")
    zz, yy = row // Y, lax.rem(row, Y)

    def on_expert(o):
        return (row, lax.rem(col + o, GROUP))

    def on_z(q):
        return (lax.rem(zz + q, Z) * Y + yy, col)

    def on_y(o):
        return (zz * Y + lax.rem(yy + o + Y, Y), col)

    right, left = on_y(1), on_y(-1)

    def remote(src, dst, send, recv, device):
        return pltpu.make_async_remote_copy(
            src_ref=src, dst_ref=dst, send_sem=send, recv_sem=recv,
            device_id=device, device_id_type=MESH,
        )

    barrier = pltpu.get_barrier_semaphore()

    @pl.loop(1, GROUP)
    def _(o):
        pl.semaphore_signal(barrier, inc=1, device_id=on_expert(o), device_id_type=MESH)

    for q in range(1, Z):
        pl.semaphore_signal(barrier, inc=1, device_id=on_z(q), device_id_type=MESH)
    pl.semaphore_signal(barrier, inc=1, device_id=right, device_id_type=MESH)
    pl.semaphore_signal(barrier, inc=1, device_id=left, device_id_type=MESH)
    pl.semaphore_wait(barrier, GROUP - 1 + Z - 1 + 2)

    def piece_out(o):
        there = on_expert(o)
        return remote(pieces_ref.at[there[1]], landed.at[col], send_x.at[o], recv_x.at[o], there)

    @pl.loop(1, GROUP)
    def _(o):
        piece_out(o).start()

    landed[col] = pieces_ref[col]

    @pl.loop(1, GROUP)
    def _(o):
        piece_out(o).wait_recv()

    size = GROUP * PIECE
    r = lax.broadcasted_iota(jnp.int32, (size, size), 0)
    c = lax.broadcasted_iota(jnp.int32, (size, size), 1)
    home = ((r >> 1) & 15) * 16 + (r >> 5) * 2 + (r & 1)
    turn = (c == home).astype(jnp.bfloat16)
    block = jnp.dot(
        turn, landed[...].reshape(size, HALF), preferred_element_type=jnp.float32
    ).astype(jnp.bfloat16)
    for h in range(2):
        for t in range(2):
            for s in range(2):
                k = ((h * 2 + t) * 2 + s) * 32
                rows[zz, yy, t, s, :, h * HALF : (h + 1) * HALF] = block[k : k + 32]

    def place(q):
        return lax.rem(zz - q + Z, Z)

    def along_z(q):
        mine = rows.at[zz, yy]
        return remote(mine, mine, send_z.at[q], recv_z.at[q], on_z(q))

    def along_y(q, d):
        mine = rows.at[place(q), yy]
        return remote(mine, mine, send_y.at[q, d], recv_y.at[q, d], left if d else right)

    def onward(q, d):
        ours = rows.at[place(q), lax.rem(yy + (1 if d else Y - 1), Y), d]
        return remote(ours, ours, send_h.at[q, d], recv_h.at[q, d], left if d else right)

    def experts(q):
        p = place(q)
        for s in range(2):
            x = rows[p, :, 0, s].reshape(Y * 32, D)
            g = rows[p, :, 1, s].reshape(Y * 32, D)
            pre_act = jnp.dot(x, w_in_ref[s], preferred_element_type=jnp.float32)
            act_grad = lax.dot_general(
                g, w_out_ref[s], (((1,), (1,)), ((), ())), preferred_element_type=jnp.float32
            )
            cdf = 0.5 * (1.0 + lax.erf(pre_act * INV_ROOT2))
            hidden = (pre_act * cdf).astype(jnp.bfloat16)
            slope = cdf + pre_act * jnp.exp(-0.5 * pre_act * pre_act) * INV_ROOT_TWO_PI
            pre_grad = (act_grad * slope).astype(jnp.bfloat16)
            hid[s, p] = hidden
            pre[s, p] = pre_grad
            out = jnp.dot(hidden, w_out_ref[s], preferred_element_type=jnp.float32)
            part[p, :, 0, s] = out.astype(jnp.bfloat16).reshape(Y, 32, D)
            back = lax.dot_general(
                pre_grad, w_in_ref[s], (((1,), (1,)), ((), ())), preferred_element_type=jnp.float32
            )
            part[p, :, 1, s] = back.astype(jnp.bfloat16).reshape(Y, 32, D)

    def far(q, d):
        ours = part.at[place(q), lax.rem(yy + 2, Y), d]
        land = (from_right if d else from_left).at[q]
        return remote(ours, land, send_f.at[q, d], recv_f.at[q, d], left if d else right)

    def near(q, d):
        ours = part.at[place(q), lax.rem(yy + (Y - 1 if d else 1), Y)]
        land = (sum_right if d else sum_left).at[q]
        return remote(ours, land, send_p.at[q, d], recv_p.at[q, d], left if d else right)

    def along_z_back(q):
        there = (place(q) * Y + yy, col)
        return remote(part.at[place(q), yy], sum_z.at[q], send_s.at[q], recv_s.at[q], there)

    def add(target, other):
        total = target[...].astype(jnp.float32) + other[...].astype(jnp.float32)
        target[...] = total.astype(jnp.bfloat16)

    def pass_on(q):
        for d in range(2):
            far(q, d).wait_recv()
            far(q, d).wait_send()
            ours = part.at[place(q), lax.rem(yy + (Y - 1 if d else 1), Y), d]
            add(ours, (from_right if d else from_left).at[q])
            near(q, d).start()

    def collect(q):
        for d in range(2):
            near(q, d).wait_recv()
        target = part.at[place(q), yy]
        total = (
            target[...].astype(jnp.float32)
            + sum_left[q].astype(jnp.float32)
            + sum_right[q].astype(jnp.float32)
        )
        target[...] = total.astype(jnp.bfloat16)
        if q > 0:
            along_z_back(q).start()

    for q in range(1, Z):
        along_z(q).start()
    for d in range(2):
        along_y(0, d).start()

    order = (0, 1, 2, 3)
    for step in range(Z):
        if step + 1 < Z:
            along_z(step + 1).wait_recv()
            for d in range(2):
                along_y(step + 1, d).start()
        for d in range(2):
            along_y(step, d).wait_recv()
            onward(step, d).start()
        for d in range(2):
            onward(step, d).wait_recv()
        experts(step)
        for d in range(2):
            far(step, d).start()
        if step >= 1:
            pass_on(step - 1)
        if step >= 2:
            collect(step - 2)

    def weights():
        for s in range(2):
            p_all = pre[s].reshape(Z * Y * 32, HID)
            h_all = hid[s].reshape(Z * Y * 32, HID)
            for k in range(0, D, 256):
                x = rows[:, :, 0, s, :, k : k + 256].reshape(Z * Y * 32, 256)
                g = rows[:, :, 1, s, :, k : k + 256].reshape(Z * Y * 32, 256)
                grad_in_ref[s, k : k + 256, :] = lax.dot_general(
                    x, p_all, (((0,), (0,)), ((), ())), preferred_element_type=jnp.float32
                ).astype(jnp.bfloat16)
                grad_out_ref[s, :, k : k + 256] = lax.dot_general(
                    h_all, g, (((0,), (0,)), ((), ())), preferred_element_type=jnp.float32
                ).astype(jnp.bfloat16)

    weights()
    pass_on(Z - 1)
    collect(Z - 2)
    collect(Z - 1)

    for q in range(1, Z):
        along_z_back(q).wait_recv()
    mine = part.at[zz, yy]
    total = mine[...].astype(jnp.float32)
    for q in range(1, Z):
        total = total + sum_z[q].astype(jnp.float32)
    total = total.astype(jnp.bfloat16)
    stack = jnp.concatenate(
        [
            total[t, s, :, h * HALF : (h + 1) * HALF]
            for h in range(2)
            for t in range(2)
            for s in range(2)
        ],
        axis=0,
    )
    home = (r & 1) * 1 + (r >> 4) * 2 + ((r >> 1) & 7) * 32
    turn = (c == home).astype(jnp.bfloat16)
    ready[...] = (
        jnp.dot(turn, stack, preferred_element_type=jnp.float32)
        .astype(jnp.bfloat16)
        .reshape(GROUP, PIECE, HALF)
    )

    def piece_back(o):
        there = on_expert(o)
        return remote(ready.at[there[1]], back_ref.at[col], send_b.at[o], recv_b.at[o], there)

    @pl.loop(1, GROUP)
    def _(o):
        piece_back(o).start()

    back_ref[col] = ready[col]

    @pl.loop(1, GROUP)
    def _(o):
        piece_back(o).wait_recv()

    @pl.loop(1, GROUP)
    def _(o):
        piece_out(o).wait_send()
        piece_back(o).wait_send()

    for q in range(Z):
        if q > 0:
            along_z(q).wait_send()
            along_z_back(q).wait_send()
        for d in range(2):
            along_y(q, d).wait_send()
            onward(q, d).wait_send()
            near(q, d).wait_send()


def expert_exchange(pieces, w_in, w_out):
    block = (2, 2, 32, D)
    bf16 = jnp.bfloat16
    dma = pltpu.SemaphoreType.DMA
    vmem = pl.BlockSpec(memory_space=pltpu.VMEM)
    return pl.pallas_call(
        exchange_kernel,
        out_shape=(
            jax.ShapeDtypeStruct(pieces.shape, bf16),
            jax.ShapeDtypeStruct(w_in.shape, bf16),
            jax.ShapeDtypeStruct(w_out.shape, bf16),
        ),
        in_specs=[vmem] * 3,
        out_specs=(vmem,) * 3,
        scratch_shapes=[
            pltpu.VMEM(pieces.shape, bf16),
            pltpu.VMEM((Z, Y) + block, bf16),
            pltpu.VMEM((Z, Y) + block, bf16),
            pltpu.VMEM((2, Z, Y * 32, HID), bf16),
            pltpu.VMEM((2, Z, Y * 32, HID), bf16),
            pltpu.VMEM((Z,) + block[1:], bf16),
            pltpu.VMEM((Z,) + block[1:], bf16),
            pltpu.VMEM((Z,) + block, bf16),
            pltpu.VMEM((Z,) + block, bf16),
            pltpu.VMEM((Z,) + block, bf16),
            pltpu.VMEM(pieces.shape, bf16),
            dma((GROUP,)), dma((GROUP,)), dma((GROUP,)), dma((GROUP,)),
            dma((Z,)), dma((Z,)),
            dma((Z, 2)), dma((Z, 2)), dma((Z, 2)), dma((Z, 2)),
            dma((Z, 2)), dma((Z, 2)), dma((Z, 2)), dma((Z, 2)),
            dma((Z,)), dma((Z,)),
        ],
        compiler_params=pltpu.CompilerParams(
            collective_id=0, has_side_effects=True, vmem_limit_bytes=56 * 1024 * 1024
        ),
        name="experts",
    )(pieces, w_in, w_out)


def local(tokens, slot_keys, w_in, w_out, grad_out):
    logits = jnp.einsum("bpd,ds->bps", tokens, slot_keys, preferred_element_type=jnp.float32)
    dispatch = jax.nn.softmax(logits, axis=1)
    combine = jax.nn.softmax(logits, axis=2)
    dispatch_low = dispatch.astype(jnp.bfloat16)
    combine_low = combine.astype(jnp.bfloat16)
    slot_in = jnp.einsum(
        "bps,bpd->bsd", dispatch_low, tokens, preferred_element_type=jnp.float32
    ).astype(jnp.bfloat16)
    slot_grad = jnp.einsum(
        "bps,bpd->bsd", combine_low, grad_out, preferred_element_type=jnp.float32
    ).astype(jnp.bfloat16)
    images, slots, width = slot_in.shape
    pieces = jnp.stack([slot_in, slot_grad]).reshape(2, images, GROUP, slots // GROUP, 2, HALF)
    pieces = pieces.transpose(2, 4, 0, 3, 1, 5).reshape(GROUP, PIECE, HALF)
    back, grad_w_in, grad_w_out = expert_exchange(pieces, w_in, w_out)
    back = back.reshape(GROUP, 2, 2, slots // GROUP, images, HALF).transpose(2, 4, 0, 3, 1, 5)
    slot_out, slot_dx = back.reshape(2, images, slots, width)
    comb_grad = jnp.einsum("bpd,bsd->bps", grad_out, slot_out, preferred_element_type=jnp.float32)
    comb_logit = combine * (comb_grad - jnp.sum(combine * comb_grad, axis=2, keepdims=True))
    disp_grad = jnp.einsum("bpd,bsd->bps", tokens, slot_dx, preferred_element_type=jnp.float32)
    disp_logit = dispatch * (disp_grad - jnp.sum(dispatch * disp_grad, axis=1, keepdims=True))
    logit_grad = (comb_logit + disp_logit).astype(jnp.bfloat16)
    grad_tokens = (
        jnp.einsum("bps,bsd->bpd", dispatch_low, slot_dx, preferred_element_type=jnp.float32)
        + jnp.einsum("bps,ds->bpd", logit_grad, slot_keys, preferred_element_type=jnp.float32)
    ).astype(jnp.bfloat16)
    key_terms = jnp.einsum("bpd,bps->sd", tokens, logit_grad, preferred_element_type=jnp.float32)
    tiles = key_terms.reshape(slots // 8, 8, width // 128, 128).transpose(0, 2, 1, 3)
    summed = sum_over_devices(tiles.reshape(-1, 8, 128))
    summed = summed.reshape(slots // 8, width // 128, 8, 128).transpose(0, 2, 1, 3)
    grad_keys = summed.reshape(slots, width).T
    return (grad_tokens, grad_keys, grad_w_in, grad_w_out)


def solution(mesh):
    return jax.shard_map(
        local,
        mesh=mesh,
        in_specs=(
            P(("dp", "expert"), None, None),
            P(),
            P("expert", None, "dp"),
            P("expert", "dp", None),
            P(("dp", "expert"), None, None),
        ),
        out_specs=(
            P(("dp", "expert"), None, None),
            P(),
            P("expert", None, "dp"),
            P("expert", "dp", None),
        ),
        check_vma=False,
    )
```

```python
import jax
import jax.numpy as jnp
from jax import lax
from jax.experimental import pallas as pl
from jax.experimental.pallas import tpu as pltpu
from jax.sharding import PartitionSpec as P

MESH = pl.DeviceIdType.MESH
GROUP = 16
Z, Y = 4, 4
D = 1280
HID = 320
HALF = D // 2
SIDE = 8
SEEN = 16
AWAY = (0, 1, 7, 2, 6, 3, 5, 4)
PIECE = 16

INV_ROOT2 = 0.7071067811865476
INV_ROOT_TWO_PI = 0.3989422804014327


def sum_kernel(x_ref, out_ref, src, landed_a, landed_b, part, total, send, recv):
    row, col = lax.axis_index("dp"), lax.axis_index("expert")

    def at(axis, offset):
        if axis == 0:
            return (lax.rem(row + offset, GROUP), col)
        return (row, lax.rem(col + offset, GROUP))

    barrier = pltpu.get_barrier_semaphore()

    @pl.loop(1, GROUP)
    def _(o):
        for axis in range(2):
            pl.semaphore_signal(barrier, inc=1, device_id=at(axis, o), device_id_type=MESH)

    tiles = x_ref.shape[0]
    src[pl.ds(0, tiles)] = x_ref[...]
    src[pl.ds(tiles, src.shape[0] - tiles)] = jnp.zeros(
        (src.shape[0] - tiles,) + src.shape[1:], src.dtype
    )
    pl.semaphore_wait(barrier, 2 * (GROUP - 1))

    def copy(round_, o):
        if round_ == 0:
            there = at(0, o)
            a, b = src.at[pl.ds(3 * there[0], 3)], landed_a.at[o]
        elif round_ == 1:
            there = at(1, o)
            a, b = part, landed_b.at[o]
        else:
            there = at(0, o)
            a, b = total, out_ref.at[row]
        return pltpu.make_async_remote_copy(
            src_ref=a,
            dst_ref=b,
            send_sem=send.at[round_, o],
            recv_sem=recv.at[round_, o],
            device_id=there,
            device_id_type=MESH,
        )

    def start(round_):
        @pl.loop(1, GROUP)
        def _(o):
            copy(round_, o).start()

    def finish(round_):
        @pl.loop(1, GROUP)
        def _(o):
            copy(round_, o).wait_recv()

    start(0)
    finish(0)
    acc = src[pl.ds(3 * row, 3)]
    for o in range(1, GROUP):
        acc = acc + landed_a[o]
    part[...] = acc
    start(1)
    finish(1)
    acc = jnp.zeros(part.shape, part.dtype)
    landed_b[0] = part[...]
    for c in range(GROUP):
        acc = acc + landed_b[lax.rem(col - c + GROUP, GROUP)]
    total[...] = acc
    start(2)
    out_ref[row] = acc
    finish(2)

    @pl.loop(1, GROUP)
    def _(o):
        for r in range(3):
            copy(r, o).wait_send()


def sum_over_devices(x):
    chunk = (3, 8, 128)
    out = pl.pallas_call(
        sum_kernel,
        out_shape=jax.ShapeDtypeStruct((GROUP,) + chunk, jnp.float32),
        in_specs=[pl.BlockSpec(memory_space=pltpu.VMEM)],
        out_specs=pl.BlockSpec(memory_space=pltpu.VMEM),
        scratch_shapes=[
            pltpu.VMEM((3 * GROUP, 8, 128), jnp.float32),
            pltpu.VMEM((GROUP,) + chunk, jnp.float32),
            pltpu.VMEM((GROUP,) + chunk, jnp.float32),
            pltpu.VMEM(chunk, jnp.float32),
            pltpu.VMEM(chunk, jnp.float32),
            pltpu.SemaphoreType.DMA((3, GROUP)),
            pltpu.SemaphoreType.DMA((3, GROUP)),
        ],
        compiler_params=pltpu.CompilerParams(collective_id=1, has_side_effects=True),
        name="sum_keys",
    )(x)
    return out.reshape(3 * GROUP, 8, 128)[: x.shape[0]]


def exchange_kernel(
    pieces_ref, w_in_ref, w_out_ref,
    back_ref, grad_in_ref, grad_out_ref,
    landed, own, rows, part, hid, pre, from_left, from_right, sum_left, sum_right, sum_z, ready,
    send_x, recv_x, send_b, recv_b, send_z, recv_z, send_s, recv_s,
    send_y, recv_y, send_h, recv_h, send_f, recv_f, send_p, recv_p,
):
    row, col = lax.axis_index("dp"), lax.axis_index("expert")
    yy = lax.rem(row, Y)
    zz = lax.rem(col // 2, 2) * Z + row // Y
    side = (col // 4) * 2 + lax.rem(col, 2)

    def on_side(o):
        p = lax.rem(side + o, SIDE)
        return p, (row, (p // 2) * 4 + lax.rem(col // 2, 2) * 2 + lax.rem(p, 2))

    def on_z(p):
        return (lax.rem(p, Z) * Y + yy, (col // 4) * 4 + (p // Z) * 2 + lax.rem(col, 2))

    def on_y(o):
        return ((row // Y) * Y + lax.rem(yy + o + Y, Y), col)

    right, left = on_y(1), on_y(-1)

    def remote(src, dst, send, recv, device):
        return pltpu.make_async_remote_copy(
            src_ref=src, dst_ref=dst, send_sem=send, recv_sem=recv,
            device_id=device, device_id_type=MESH,
        )

    barrier = pltpu.get_barrier_semaphore()
    for o in range(1, SIDE):
        pl.semaphore_signal(barrier, inc=1, device_id=on_side(o)[1], device_id_type=MESH)
        pl.semaphore_signal(
            barrier, inc=1, device_id=on_z(lax.rem(zz + o, 2 * Z)), device_id_type=MESH
        )
    pl.semaphore_signal(barrier, inc=1, device_id=right, device_id_type=MESH)
    pl.semaphore_signal(barrier, inc=1, device_id=left, device_id_type=MESH)
    pl.semaphore_wait(barrier, 2 * (SIDE - 1) + 2)

    def piece_out(o):
        p, there = on_side(o)
        return remote(pieces_ref.at[p], landed.at[side], send_x.at[o], recv_x.at[o], there)

    for o in range(1, SIDE):
        piece_out(o).start()
    landed[side] = pieces_ref[side]

    size = SIDE * PIECE
    r = lax.broadcasted_iota(jnp.int32, (size, size), 0)
    c = lax.broadcasted_iota(jnp.int32, (size, size), 1)
    turn = (c == ((r >> 1) & 7) * 16 + (r >> 4) * 2 + (r & 1)).astype(jnp.bfloat16)

    def turned(x):
        return jnp.dot(turn, x, preferred_element_type=jnp.float32).astype(jnp.bfloat16)

    parts_of_piece = [(h, t, s) for h in range(2) for t in range(2) for s in range(2)]
    for o in range(1, SIDE):
        piece_out(o).wait_recv()
    for g in range(2):
        block = turned(landed[:, g].reshape(size, HALF))
        for k, (h, t, s) in enumerate(parts_of_piece):
            own[g, t, s, :, h * HALF : (h + 1) * HALF] = block[k * SEEN : (k + 1) * SEEN]

    def place(q):
        return lax.rem(zz - AWAY[q] + 2 * Z, 2 * Z)

    def along_z(q):
        p = lax.rem(zz + AWAY[q], 2 * Z)
        return remote(own.at[p // Z], rows.at[zz, yy], send_z.at[q], recv_z.at[q], on_z(p))

    def along_y(q, d):
        mine = rows.at[place(q), yy]
        return remote(mine, mine, send_y.at[q, d], recv_y.at[q, d], left if d else right)

    def onward(q, d):
        ours = rows.at[place(q), lax.rem(yy + (1 if d else Y - 1), Y), d]
        return remote(ours, ours, send_h.at[q, d], recv_h.at[q, d], left if d else right)

    def times(a, b, over):
        return lax.dot_general(a, b, (over, ((), ())), preferred_element_type=jnp.float32)

    def experts(q):
        p = place(q)
        for s in range(2):
            x = rows[p, :, 0, s].reshape(Y * SEEN, D)
            g = rows[p, :, 1, s].reshape(Y * SEEN, D)
            pre_act = times(x, w_in_ref[s], ((1,), (1,)))
            act_grad = times(g, w_out_ref[s], ((1,), (1,)))
            cdf = 0.5 * (1.0 + lax.erf(pre_act * INV_ROOT2))
            hidden = (pre_act * cdf).astype(jnp.bfloat16)
            slope = cdf + pre_act * jnp.exp(-0.5 * pre_act * pre_act) * INV_ROOT_TWO_PI
            pre_grad = (act_grad * slope).astype(jnp.bfloat16)
            hid[s, p] = hidden
            pre[s, p] = pre_grad
            out = times(hidden, w_out_ref[s], ((1,), (0,)))
            part[p, :, 0, s] = out.astype(jnp.bfloat16).reshape(Y, SEEN, D)
            back = times(pre_grad, w_in_ref[s], ((1,), (0,)))
            part[p, :, 1, s] = back.astype(jnp.bfloat16).reshape(Y, SEEN, D)

    def far(q, d):
        ours = part.at[place(q), lax.rem(yy + 2, Y), d]
        land = (from_right if d else from_left).at[q]
        return remote(ours, land, send_f.at[q, d], recv_f.at[q, d], left if d else right)

    def near(q, d):
        ours = part.at[place(q), lax.rem(yy + (Y - 1 if d else 1), Y)]
        land = (sum_right if d else sum_left).at[q]
        return remote(ours, land, send_p.at[q, d], recv_p.at[q, d], left if d else right)

    def along_z_back(q):
        p = place(q)
        return remote(part.at[p, yy], sum_z.at[zz], send_s.at[q], recv_s.at[q], on_z(p))

    def begin(q):
        for d in range(2):
            far(q, d).start()

    def pass_on(q):
        for d in range(2):
            far(q, d).wait_recv()
            ours = part.at[place(q), lax.rem(yy + (Y - 1 if d else 1), Y), d]
            other = (from_right if d else from_left)[q].astype(jnp.float32)
            ours[...] = (ours[...].astype(jnp.float32) + other).astype(jnp.bfloat16)
            near(q, d).start()

    def collect(q):
        for d in range(2):
            near(q, d).wait_recv()
        total = (
            part[place(q), yy].astype(jnp.float32)
            + sum_left[q].astype(jnp.float32)
            + sum_right[q].astype(jnp.float32)
        ).astype(jnp.bfloat16)
        if q == 0:
            sum_z[zz] = total
        else:
            part[place(q), yy] = total
            along_z_back(q).start()

    last = len(AWAY) - 1
    for q in range(1, 4):
        along_z(q).start()
    rows[zz, yy] = own[zz // Z]

    def fetch(q):
        if 1 <= q <= last:
            along_z(q).wait_recv()
            if q + 3 <= last:
                along_z(q + 3).start()
        if q <= last:
            for d in range(2):
                along_y(q, d).start()

    def spread(q):
        if q <= last:
            for d in range(2):
                along_y(q, d).wait_recv()
                onward(q, d).start()

    fetch(0)
    fetch(1)
    spread(0)
    for q in range(last + 1):
        fetch(q + 2)
        spread(q + 1)
        for d in range(2):
            onward(q, d).wait_recv()
        experts(q)
        if q >= 1:
            begin(q)
        if q >= 2:
            pass_on(q - 1)
        if q >= 3:
            collect(q - 2)
    begin(0)

    for s in range(2):
        p_all = pre[s].reshape(2 * Z * Y * SEEN, HID)
        h_all = hid[s].reshape(2 * Z * Y * SEEN, HID)
        for k in range(0, D, 256):
            x = rows[:, :, 0, s, :, k : k + 256].reshape(2 * Z * Y * SEEN, 256)
            g = rows[:, :, 1, s, :, k : k + 256].reshape(2 * Z * Y * SEEN, 256)
            grad_in_ref[s, :, k : k + 256] = times(p_all, x, ((0,), (0,))).astype(jnp.bfloat16)
            grad_out_ref[s, :, k : k + 256] = times(h_all, g, ((0,), (0,))).astype(jnp.bfloat16)
        if s == 0:
            pass_on(last)
            collect(last - 1)
            pass_on(0)
    collect(last)
    collect(0)

    for q in range(1, last + 1):
        along_z_back(q).wait_recv()
    for g in range(2):
        total = sum_z[g * Z].astype(jnp.float32)
        for k in range(1, Z):
            total = total + sum_z[g * Z + k].astype(jnp.float32)
        total = total.astype(jnp.bfloat16)
        stack = jnp.concatenate(
            [total[t, s, :, h * HALF : (h + 1) * HALF] for h, t, s in parts_of_piece], axis=0
        )
        ready[:, g] = turned(stack).reshape(SIDE, PIECE, HALF)

    def piece_back(o):
        p, there = on_side(o)
        return remote(ready.at[p], back_ref.at[side], send_b.at[o], recv_b.at[o], there)

    for o in range(1, SIDE):
        piece_back(o).start()
    back_ref[side] = ready[side]
    for o in range(1, SIDE):
        piece_back(o).wait_recv()

    for o in range(1, SIDE):
        piece_out(o).wait_send()
        piece_back(o).wait_send()
    for q in range(last + 1):
        if q > 0:
            along_z(q).wait_send()
            along_z_back(q).wait_send()
        for d in range(2):
            along_y(q, d).wait_send()
            onward(q, d).wait_send()
            far(q, d).wait_send()
            near(q, d).wait_send()


def expert_exchange(pieces, w_in_turned, w_out):
    block = (2, 2, SEEN, D)
    slabs = 2 * Z
    bf16 = jnp.bfloat16
    dma = pltpu.SemaphoreType.DMA
    vmem = pl.BlockSpec(memory_space=pltpu.VMEM)
    return pl.pallas_call(
        exchange_kernel,
        out_shape=(
            jax.ShapeDtypeStruct(pieces.shape, bf16),
            jax.ShapeDtypeStruct(w_out.shape, bf16),
            jax.ShapeDtypeStruct(w_out.shape, bf16),
        ),
        in_specs=[vmem] * 3,
        out_specs=(vmem,) * 3,
        scratch_shapes=[
            pltpu.VMEM(pieces.shape, bf16),
            pltpu.VMEM((2,) + block, bf16),
            pltpu.VMEM((slabs, Y) + block, bf16),
            pltpu.VMEM((slabs, Y) + block, bf16),
            pltpu.VMEM((2, slabs, Y * SEEN, HID), bf16),
            pltpu.VMEM((2, slabs, Y * SEEN, HID), bf16),
            pltpu.VMEM((slabs,) + block[1:], bf16),
            pltpu.VMEM((slabs,) + block[1:], bf16),
            pltpu.VMEM((slabs,) + block, bf16),
            pltpu.VMEM((slabs,) + block, bf16),
            pltpu.VMEM((slabs,) + block, bf16),
            pltpu.VMEM(pieces.shape, bf16),
        ]
        + [dma((SIDE,))] * 8
        + [dma((slabs, 2))] * 8,
        compiler_params=pltpu.CompilerParams(
            collective_id=0, has_side_effects=True, vmem_limit_bytes=56 * 1024 * 1024
        ),
        name="experts",
    )(pieces, w_in_turned, w_out)


def local(tokens, slot_keys, w_in, w_out, grad_out):
    logits = jnp.einsum("bpd,ds->bps", tokens, slot_keys, preferred_element_type=jnp.float32)
    dispatch = jax.nn.softmax(logits, axis=1)
    combine = jax.nn.softmax(logits, axis=2)
    dispatch_low = dispatch.astype(jnp.bfloat16)
    combine_low = combine.astype(jnp.bfloat16)
    slot_in = jnp.einsum(
        "bps,bpd->bsd", dispatch_low, tokens, preferred_element_type=jnp.float32
    ).astype(jnp.bfloat16)
    slot_grad = jnp.einsum(
        "bps,bpd->bsd", combine_low, grad_out, preferred_element_type=jnp.float32
    ).astype(jnp.bfloat16)
    images, slots, width = slot_in.shape
    pieces = jnp.stack([slot_in, slot_grad]).reshape(2, images, 4, 2, 2, slots // GROUP, 2, HALF)
    pieces = pieces.transpose(2, 4, 3, 6, 0, 5, 1, 7).reshape(SIDE, 2, PIECE, HALF)
    back, grad_w_in, grad_w_out = expert_exchange(pieces, w_in.transpose(0, 2, 1), w_out)
    grad_w_in = grad_w_in.transpose(0, 2, 1)
    back = back.reshape(4, 2, 2, 2, 2, slots // GROUP, images, HALF)
    back = back.transpose(4, 6, 0, 2, 1, 5, 3, 7)
    slot_out, slot_dx = back.reshape(2, images, slots, width)
    comb_grad = jnp.einsum("bpd,bsd->bps", grad_out, slot_out, preferred_element_type=jnp.float32)
    comb_logit = combine * (comb_grad - jnp.sum(combine * comb_grad, axis=2, keepdims=True))
    disp_grad = jnp.einsum("bpd,bsd->bps", tokens, slot_dx, preferred_element_type=jnp.float32)
    disp_logit = dispatch * (disp_grad - jnp.sum(dispatch * disp_grad, axis=1, keepdims=True))
    logit_grad = (comb_logit + disp_logit).astype(jnp.bfloat16)
    grad_tokens = (
        jnp.einsum("bps,bsd->bpd", dispatch_low, slot_dx, preferred_element_type=jnp.float32)
        + jnp.einsum("bps,ds->bpd", logit_grad, slot_keys, preferred_element_type=jnp.float32)
    ).astype(jnp.bfloat16)
    key_terms = jnp.einsum("bpd,bps->sd", tokens, logit_grad, preferred_element_type=jnp.float32)
    tiles = key_terms.reshape(slots // 8, 8, width // 128, 128).transpose(0, 2, 1, 3)
    summed = sum_over_devices(tiles.reshape(-1, 8, 128))
    summed = summed.reshape(slots // 8, width // 128, 8, 128).transpose(0, 2, 1, 3)
    grad_keys = summed.reshape(slots, width).T
    return (grad_tokens, grad_keys, grad_w_in, grad_w_out)


def solution(mesh):
    return jax.shard_map(
        local,
        mesh=mesh,
        in_specs=(
            P(("dp", "expert"), None, None),
            P(),
            P("expert", None, "dp"),
            P("expert", "dp", None),
            P(("dp", "expert"), None, None),
        ),
        out_specs=(
            P(("dp", "expert"), None, None),
            P(),
            P("expert", None, "dp"),
            P("expert", "dp", None),
        ),
        check_vma=False,
    )
```

```python
import jax
import jax.numpy as jnp
from jax import lax
from jax.experimental import pallas as pl
from jax.experimental.pallas import tpu as pltpu
from jax.sharding import PartitionSpec as P

MESH = pl.DeviceIdType.MESH
GROUP = 16
Z, Y = 4, 4
D = 1280
HID = 320
HALF = D // 2
SLOTS = 32
TILES = D // 128
SIDE = 8
SEEN = 16
AWAY = (0, 1, 7, 2, 6, 3, 5, 4)
PIECE = 16

INV_ROOT2 = 0.7071067811865476
INV_ROOT_TWO_PI = 0.3989422804014327


def times(a, b, over):
    return lax.dot_general(a, b, (over, ((), ())), preferred_element_type=jnp.float32)


def soft(x, axis):
    e = jnp.exp(x - jnp.max(x, axis=axis, keepdims=True))
    return e / jnp.sum(e, axis=axis, keepdims=True)


def combine_kernel(
    tokens_ref, grad_ref, keys_ref, back_ref, dx_ref, keys_out_ref,
    terms, other, chunks, landed, part, parts_z, total, done, done_other,
    send_c, recv_c, send_a, recv_a, send_z, recv_z, send_d, recv_d,
):
    row, col = lax.axis_index("dp"), lax.axis_index("expert")
    xx, yy, core = col // 4, lax.rem(row, Y), lax.rem(col, 2)
    half_z = lax.rem(col // 2, 2)
    zz = half_z * Z + row // Y
    flat = xx * Y + yy

    def on_plane(p):
        return ((row // Y) * Y + lax.rem(p, Y), (p // Y) * 4 + half_z * 2 + core)

    def on_z(p):
        return (lax.rem(p, Z) * Y + yy, xx * 4 + (p // Z) * 2 + core)

    twin = (row, col - core + 1 - core)

    def remote(src, dst, send, recv, device):
        return pltpu.make_async_remote_copy(
            src_ref=src, dst_ref=dst, send_sem=send, recv_sem=recv,
            device_id=device, device_id_type=MESH,
        )

    barrier = pltpu.get_barrier_semaphore()
    pl.semaphore_signal(barrier, inc=1, device_id=twin, device_id_type=MESH)
    for o in range(1, GROUP):
        p = lax.rem(flat + o, GROUP)
        pl.semaphore_signal(barrier, inc=1, device_id=on_plane(p), device_id_type=MESH)
    for o in range(1, 2 * Z):
        p = lax.rem(zz + o, 2 * Z)
        pl.semaphore_signal(barrier, inc=1, device_id=on_z(p), device_id_type=MESH)

    size = GROUP * PIECE
    r = lax.broadcasted_iota(jnp.int32, (size, size), 0)
    c = lax.broadcasted_iota(jnp.int32, (size, size), 1)
    home = ((r >> 3) & 3) * 64 + ((r >> 1) & 1) * 32 + ((r >> 2) & 1) * 16
    home = home + (r >> 7) * 8 + ((r >> 6) & 1) * 4 + (r & 1) * 2 + ((r >> 5) & 1)
    turn = (c == home).astype(jnp.bfloat16)
    slots = times(turn, back_ref[...].reshape(size, HALF), ((1,), (0,))).astype(jnp.bfloat16)

    def slot_rows(t, i):
        k = (t * 2 + i) * SLOTS
        return jnp.concatenate(
            [slots[h * 4 * SLOTS + k : h * 4 * SLOTS + k + SLOTS] for h in range(2)], axis=1
        )

    keys = keys_ref[...]
    weights, sums = [], None
    for i in range(2):
        slot_out, slot_dx = slot_rows(0, i), slot_rows(1, i)
        both = times(jnp.concatenate([keys, slot_dx], axis=0), tokens_ref[i], ((1,), (1,)))
        logits, disp_grad = both[:SLOTS], both[SLOTS:]
        dispatch, combine = soft(logits, 1), soft(logits, 0)
        comb_grad = times(slot_out, grad_ref[i], ((1,), (1,)))
        inner = jnp.sum(combine * comb_grad, axis=0, keepdims=True)
        comb_logit = combine * (comb_grad - inner)
        inner = jnp.sum(dispatch * disp_grad, axis=1, keepdims=True)
        disp_logit = dispatch * (disp_grad - inner)
        logit_grad = (comb_logit + disp_logit).astype(jnp.bfloat16)
        term = times(logit_grad, tokens_ref[i], ((1,), (0,)))
        sums = term if sums is None else sums + term
        weights.append(
            (
                jnp.concatenate([dispatch.astype(jnp.bfloat16), logit_grad], axis=0),
                jnp.concatenate([slot_dx, keys], axis=0),
            )
        )

    def token_grads(i):
        a, b = weights[i]
        dx_ref[i] = times(a, b, ((0,), (0,))).astype(jnp.bfloat16)

    for h in range(2):
        terms[h] = sums[h * SLOTS // 2 : (h + 1) * SLOTS // 2]
    pl.semaphore_wait(barrier, 1 + GROUP - 1 + 2 * Z - 1)
    to_twin = remote(terms.at[1 - core], other, send_c.at[0], recv_c.at[0], twin)
    to_twin.start()
    token_grads(0)
    to_twin.wait_recv()
    mine = terms[core] + other[...]
    for k in range(TILES):
        chunks[k] = mine[:, k * 128 : (k + 1) * 128]

    def to_owner(o):
        p = lax.rem(flat + o, GROUP)
        return remote(chunks.at[p], landed.at[o], send_a.at[o], recv_a.at[o], on_plane(p))

    def from_owner(o):
        p = lax.rem(flat + o, GROUP)
        return remote(total, done.at[flat], send_d.at[o], recv_d.at[o], on_plane(p))

    def across_z(o):
        p = lax.rem(zz + o, 2 * Z)
        return remote(part, parts_z.at[zz], send_z.at[o], recv_z.at[o], on_z(p))

    owner = flat < TILES
    for o in range(1, GROUP):

        @pl.when(lax.rem(flat + o, GROUP) < TILES)
        def _():
            to_owner(o).start()

    token_grads(1)

    @pl.when(owner)
    def _():
        acc = chunks[flat]
        for o in range(1, GROUP):
            to_owner(o).wait_recv()
            acc = acc + landed[o]
        part[...] = acc
        for o in range(1, 2 * Z):
            across_z(o).start()
        parts_z[zz] = acc
        for o in range(1, 2 * Z):
            across_z(o).wait_recv()
        acc = parts_z[0]
        for k in range(1, 2 * Z):
            acc = acc + parts_z[k]
        total[...] = acc
        for o in range(1, GROUP):
            from_owner(o).start()
        done[flat] = acc

    for o in range(1, GROUP):

        @pl.when(lax.rem(flat - o + GROUP, GROUP) < TILES)
        def _():
            from_owner(o).wait_recv()

    back_to_twin = remote(done.at[pl.ds(0, TILES)], done_other, send_c.at[1], recv_c.at[1], twin)
    back_to_twin.start()
    first = pl.ds(pl.multiple_of(core * (SLOTS // 2), SLOTS // 2), SLOTS // 2)
    second = pl.ds(pl.multiple_of((1 - core) * (SLOTS // 2), SLOTS // 2), SLOTS // 2)
    for k in range(TILES):
        keys_out_ref[first, k * 128 : (k + 1) * 128] = done[k]
    back_to_twin.wait_recv()
    for k in range(TILES):
        keys_out_ref[second, k * 128 : (k + 1) * 128] = done_other[k]

    to_twin.wait_send()
    back_to_twin.wait_send()
    for o in range(1, GROUP):

        @pl.when(lax.rem(flat + o, GROUP) < TILES)
        def _():
            to_owner(o).wait_send()

    @pl.when(owner)
    def _():
        for o in range(1, GROUP):
            from_owner(o).wait_send()
        for o in range(1, 2 * Z):
            across_z(o).wait_send()


def combine_gradients(tokens, grad_out, keys_turned, back):
    f32 = jnp.float32
    dma = pltpu.SemaphoreType.DMA
    vmem = pl.BlockSpec(memory_space=pltpu.VMEM)
    tile = (SLOTS // 2, 128)
    return pl.pallas_call(
        combine_kernel,
        out_shape=(
            jax.ShapeDtypeStruct(tokens.shape, jnp.bfloat16),
            jax.ShapeDtypeStruct(keys_turned.shape, f32),
        ),
        in_specs=[vmem] * 4,
        out_specs=(vmem,) * 2,
        scratch_shapes=[
            pltpu.VMEM((2, SLOTS // 2, D), f32),
            pltpu.VMEM((SLOTS // 2, D), f32),
            pltpu.VMEM((GROUP,) + tile, f32),
            pltpu.VMEM((GROUP,) + tile, f32),
            pltpu.VMEM(tile, f32),
            pltpu.VMEM((2 * Z,) + tile, f32),
            pltpu.VMEM(tile, f32),
            pltpu.VMEM((GROUP,) + tile, f32),
            pltpu.VMEM((TILES,) + tile, f32),
            dma((2,)), dma((2,)),
            dma((GROUP,)), dma((GROUP,)),
            dma((2 * Z,)), dma((2 * Z,)),
            dma((GROUP,)), dma((GROUP,)),
        ],
        compiler_params=pltpu.CompilerParams(
            collective_id=1, has_side_effects=True, vmem_limit_bytes=48 * 1024 * 1024
        ),
        name="combine",
    )(tokens, grad_out, keys_turned, back)


def exchange_kernel(
    pieces_ref, w_in_ref, w_out_ref,
    back_ref, grad_in_ref, grad_out_ref,
    landed, own, rows, part, hid, pre, from_left, from_right, sum_left, sum_right, sum_z, ready,
    send_x, recv_x, send_b, recv_b, send_z, recv_z, send_s, recv_s,
    send_y, recv_y, send_h, recv_h, send_f, recv_f, send_p, recv_p,
):
    row, col = lax.axis_index("dp"), lax.axis_index("expert")
    yy = lax.rem(row, Y)
    zz = lax.rem(col // 2, 2) * Z + row // Y
    side = (col // 4) * 2 + lax.rem(col, 2)

    def on_side(o):
        p = lax.rem(side + o, SIDE)
        return p, (row, (p // 2) * 4 + lax.rem(col // 2, 2) * 2 + lax.rem(p, 2))

    def on_z(p):
        return (lax.rem(p, Z) * Y + yy, (col // 4) * 4 + (p // Z) * 2 + lax.rem(col, 2))

    def on_y(o):
        return ((row // Y) * Y + lax.rem(yy + o + Y, Y), col)

    right, left = on_y(1), on_y(-1)

    def remote(src, dst, send, recv, device):
        return pltpu.make_async_remote_copy(
            src_ref=src, dst_ref=dst, send_sem=send, recv_sem=recv,
            device_id=device, device_id_type=MESH,
        )

    barrier = pltpu.get_barrier_semaphore()
    for o in range(1, SIDE):
        pl.semaphore_signal(barrier, inc=1, device_id=on_side(o)[1], device_id_type=MESH)
        pl.semaphore_signal(
            barrier, inc=1, device_id=on_z(lax.rem(zz + o, 2 * Z)), device_id_type=MESH
        )
    pl.semaphore_signal(barrier, inc=1, device_id=right, device_id_type=MESH)
    pl.semaphore_signal(barrier, inc=1, device_id=left, device_id_type=MESH)
    pl.semaphore_wait(barrier, 2 * (SIDE - 1) + 2)

    def piece_out(o):
        p, there = on_side(o)
        return remote(pieces_ref.at[p], landed.at[side], send_x.at[o], recv_x.at[o], there)

    for o in range(1, SIDE):
        piece_out(o).start()
    landed[side] = pieces_ref[side]

    size = SIDE * PIECE
    r = lax.broadcasted_iota(jnp.int32, (size, size), 0)
    c = lax.broadcasted_iota(jnp.int32, (size, size), 1)
    turn = (c == ((r >> 1) & 7) * 16 + (r >> 4) * 2 + (r & 1)).astype(jnp.bfloat16)

    def turned(x):
        return jnp.dot(turn, x, preferred_element_type=jnp.float32).astype(jnp.bfloat16)

    parts_of_piece = [(h, t, s) for h in range(2) for t in range(2) for s in range(2)]
    for o in range(1, SIDE):
        piece_out(o).wait_recv()
    for g in range(2):
        block = turned(landed[:, g].reshape(size, HALF))
        for k, (h, t, s) in enumerate(parts_of_piece):
            own[g, t, s, :, h * HALF : (h + 1) * HALF] = block[k * SEEN : (k + 1) * SEEN]

    def place(q):
        return lax.rem(zz - AWAY[q] + 2 * Z, 2 * Z)

    def along_z(q):
        p = lax.rem(zz + AWAY[q], 2 * Z)
        return remote(own.at[p // Z], rows.at[zz, yy], send_z.at[q], recv_z.at[q], on_z(p))

    def along_y(q, d):
        mine = rows.at[place(q), yy]
        return remote(mine, mine, send_y.at[q, d], recv_y.at[q, d], left if d else right)

    def onward(q, d):
        ours = rows.at[place(q), lax.rem(yy + (1 if d else Y - 1), Y), d]
        return remote(ours, ours, send_h.at[q, d], recv_h.at[q, d], left if d else right)

    def experts(q):
        p = place(q)
        for s in range(2):
            x = rows[p, :, 0, s].reshape(Y * SEEN, D)
            g = rows[p, :, 1, s].reshape(Y * SEEN, D)
            pre_act = times(x, w_in_ref[s], ((1,), (1,)))
            act_grad = times(g, w_out_ref[s], ((1,), (1,)))
            cdf = 0.5 * (1.0 + lax.erf(pre_act * INV_ROOT2))
            hidden = (pre_act * cdf).astype(jnp.bfloat16)
            slope = cdf + pre_act * jnp.exp(-0.5 * pre_act * pre_act) * INV_ROOT_TWO_PI
            pre_grad = (act_grad * slope).astype(jnp.bfloat16)
            hid[s, p] = hidden
            pre[s, p] = pre_grad
            out = times(hidden, w_out_ref[s], ((1,), (0,)))
            part[p, :, 0, s] = out.astype(jnp.bfloat16).reshape(Y, SEEN, D)
            back = times(pre_grad, w_in_ref[s], ((1,), (0,)))
            part[p, :, 1, s] = back.astype(jnp.bfloat16).reshape(Y, SEEN, D)

    def far(q, d):
        ours = part.at[place(q), lax.rem(yy + 2, Y), d]
        land = (from_right if d else from_left).at[q]
        return remote(ours, land, send_f.at[q, d], recv_f.at[q, d], left if d else right)

    def near(q, d):
        ours = part.at[place(q), lax.rem(yy + (Y - 1 if d else 1), Y)]
        land = (sum_right if d else sum_left).at[q]
        return remote(ours, land, send_p.at[q, d], recv_p.at[q, d], left if d else right)

    def along_z_back(q):
        p = place(q)
        return remote(part.at[p, yy], sum_z.at[zz], send_s.at[q], recv_s.at[q], on_z(p))

    def begin(q):
        for d in range(2):
            far(q, d).start()

    def pass_on(q):
        for d in range(2):
            far(q, d).wait_recv()
            ours = part.at[place(q), lax.rem(yy + (Y - 1 if d else 1), Y), d]
            other = (from_right if d else from_left)[q].astype(jnp.float32)
            ours[...] = (ours[...].astype(jnp.float32) + other).astype(jnp.bfloat16)
            near(q, d).start()

    def collect(q):
        for d in range(2):
            near(q, d).wait_recv()
        total = (
            part[place(q), yy].astype(jnp.float32)
            + sum_left[q].astype(jnp.float32)
            + sum_right[q].astype(jnp.float32)
        ).astype(jnp.bfloat16)
        if q == 0:
            sum_z[zz] = total
        else:
            part[place(q), yy] = total
            along_z_back(q).start()

    last = len(AWAY) - 1
    for q in range(1, 4):
        along_z(q).start()
    rows[zz, yy] = own[zz // Z]

    def fetch(q):
        if 1 <= q <= last:
            along_z(q).wait_recv()
            if q + 3 <= last:
                along_z(q + 3).start()
        if q <= last:
            for d in range(2):
                along_y(q, d).start()

    def spread(q):
        if q <= last:
            for d in range(2):
                along_y(q, d).wait_recv()
                onward(q, d).start()

    fetch(0)
    fetch(1)
    spread(0)
    for q in range(last + 1):
        fetch(q + 2)
        spread(q + 1)
        for d in range(2):
            onward(q, d).wait_recv()
        experts(q)
        if q >= 1:
            begin(q)
        if q >= 2:
            pass_on(q - 1)
        if q >= 3:
            collect(q - 2)
    begin(0)

    for s in range(2):
        p_all = pre[s].reshape(2 * Z * Y * SEEN, HID)
        h_all = hid[s].reshape(2 * Z * Y * SEEN, HID)
        for k in range(0, D, 256):
            x = rows[:, :, 0, s, :, k : k + 256].reshape(2 * Z * Y * SEEN, 256)
            g = rows[:, :, 1, s, :, k : k + 256].reshape(2 * Z * Y * SEEN, 256)
            grad_in_ref[s, :, k : k + 256] = times(p_all, x, ((0,), (0,))).astype(jnp.bfloat16)
            grad_out_ref[s, :, k : k + 256] = times(h_all, g, ((0,), (0,))).astype(jnp.bfloat16)
        if s == 0:
            pass_on(last)
            collect(last - 1)
            pass_on(0)
    collect(last)
    collect(0)

    for q in range(1, last + 1):
        along_z_back(q).wait_recv()
    for g in range(2):
        total = sum_z[g * Z].astype(jnp.float32)
        for k in range(1, Z):
            total = total + sum_z[g * Z + k].astype(jnp.float32)
        total = total.astype(jnp.bfloat16)
        stack = jnp.concatenate(
            [total[t, s, :, h * HALF : (h + 1) * HALF] for h, t, s in parts_of_piece], axis=0
        )
        ready[:, g] = turned(stack).reshape(SIDE, PIECE, HALF)

    def piece_back(o):
        p, there = on_side(o)
        return remote(ready.at[p], back_ref.at[side], send_b.at[o], recv_b.at[o], there)

    for o in range(1, SIDE):
        piece_back(o).start()
    back_ref[side] = ready[side]
    for o in range(1, SIDE):
        piece_back(o).wait_recv()

    for o in range(1, SIDE):
        piece_out(o).wait_send()
        piece_back(o).wait_send()
    for q in range(last + 1):
        if q > 0:
            along_z(q).wait_send()
            along_z_back(q).wait_send()
        for d in range(2):
            along_y(q, d).wait_send()
            onward(q, d).wait_send()
            far(q, d).wait_send()
            near(q, d).wait_send()


def expert_exchange(pieces, w_in_turned, w_out):
    block = (2, 2, SEEN, D)
    slabs = 2 * Z
    bf16 = jnp.bfloat16
    dma = pltpu.SemaphoreType.DMA
    vmem = pl.BlockSpec(memory_space=pltpu.VMEM)
    return pl.pallas_call(
        exchange_kernel,
        out_shape=(
            jax.ShapeDtypeStruct(pieces.shape, bf16),
            jax.ShapeDtypeStruct(w_out.shape, bf16),
            jax.ShapeDtypeStruct(w_out.shape, bf16),
        ),
        in_specs=[vmem] * 3,
        out_specs=(vmem,) * 3,
        scratch_shapes=[
            pltpu.VMEM(pieces.shape, bf16),
            pltpu.VMEM((2,) + block, bf16),
            pltpu.VMEM((slabs, Y) + block, bf16),
            pltpu.VMEM((slabs, Y) + block, bf16),
            pltpu.VMEM((2, slabs, Y * SEEN, HID), bf16),
            pltpu.VMEM((2, slabs, Y * SEEN, HID), bf16),
            pltpu.VMEM((slabs,) + block[1:], bf16),
            pltpu.VMEM((slabs,) + block[1:], bf16),
            pltpu.VMEM((slabs,) + block, bf16),
            pltpu.VMEM((slabs,) + block, bf16),
            pltpu.VMEM((slabs,) + block, bf16),
            pltpu.VMEM(pieces.shape, bf16),
        ]
        + [dma((SIDE,))] * 8
        + [dma((slabs, 2))] * 8,
        compiler_params=pltpu.CompilerParams(
            collective_id=0, has_side_effects=True, vmem_limit_bytes=56 * 1024 * 1024
        ),
        name="experts",
    )(pieces, w_in_turned, w_out)


def local(tokens, slot_keys, w_in, w_out, grad_out):
    logits = jnp.einsum("bpd,ds->bps", tokens, slot_keys, preferred_element_type=jnp.float32)
    dispatch = jax.nn.softmax(logits, axis=1)
    combine = jax.nn.softmax(logits, axis=2)
    dispatch_low = dispatch.astype(jnp.bfloat16)
    combine_low = combine.astype(jnp.bfloat16)
    slot_in = jnp.einsum(
        "bps,bpd->bsd", dispatch_low, tokens, preferred_element_type=jnp.float32
    ).astype(jnp.bfloat16)
    slot_grad = jnp.einsum(
        "bps,bpd->bsd", combine_low, grad_out, preferred_element_type=jnp.float32
    ).astype(jnp.bfloat16)
    images, slots, width = slot_in.shape
    pieces = jnp.stack([slot_in, slot_grad]).reshape(2, images, 4, 2, 2, slots // GROUP, 2, HALF)
    pieces = pieces.transpose(2, 4, 3, 6, 0, 5, 1, 7).reshape(SIDE, 2, PIECE, HALF)
    back, grad_w_in, grad_w_out = expert_exchange(pieces, w_in.transpose(0, 2, 1), w_out)
    grad_w_in = grad_w_in.transpose(0, 2, 1)
    grad_tokens, grad_keys = combine_gradients(tokens, grad_out, slot_keys.T, back)
    return (grad_tokens, grad_keys.T, grad_w_in, grad_w_out)


def solution(mesh):
    return jax.shard_map(
        local,
        mesh=mesh,
        in_specs=(
            P(("dp", "expert"), None, None),
            P(),
            P("expert", None, "dp"),
            P("expert", "dp", None),
            P(("dp", "expert"), None, None),
        ),
        out_specs=(
            P(("dp", "expert"), None, None),
            P(),
            P("expert", None, "dp"),
            P("expert", "dp", None),
        ),
        check_vma=False,
    )
```

```python
import jax
import jax.numpy as jnp
from jax import lax
from jax.experimental import pallas as pl
from jax.experimental.pallas import tpu as pltpu
from jax.sharding import PartitionSpec as P

MESH = pl.DeviceIdType.MESH
GROUP = 16
Z, Y = 4, 4
D = 1280
HID = 320
HALF = D // 2
SLOTS = 32
TILES = D // 128
SIDE = 8
SEEN = 16
AWAY = (0, 1, 7, 2, 6, 3, 5, 4)
PIECE = 16

INV_ROOT2 = 0.7071067811865476
INV_ROOT_TWO_PI = 0.3989422804014327


def times(a, b, over):
    return lax.dot_general(a, b, (over, ((), ())), preferred_element_type=jnp.float32)


def soft(x, axis):
    e = jnp.exp(x - jnp.max(x, axis=axis, keepdims=True))
    return e / jnp.sum(e, axis=axis, keepdims=True)


def combine_kernel(
    tokens_ref, grad_ref, keys_ref, back_ref, dx_ref, keys_out_ref,
    terms, other, chunks, landed, part, parts_z, total, done, done_other,
    send_c, recv_c, send_a, recv_a, send_z, recv_z, send_d, recv_d,
):
    row, col = lax.axis_index("dp"), lax.axis_index("expert")
    xx, yy, core = col // 4, lax.rem(row, Y), lax.rem(col, 2)
    half_z = lax.rem(col // 2, 2)
    zz = half_z * Z + row // Y
    flat = xx * Y + yy

    def on_plane(p):
        return ((row // Y) * Y + lax.rem(p, Y), (p // Y) * 4 + half_z * 2 + core)

    def on_z(p):
        return (lax.rem(p, Z) * Y + yy, xx * 4 + (p // Z) * 2 + core)

    twin = (row, col - core + 1 - core)

    def remote(src, dst, send, recv, device):
        return pltpu.make_async_remote_copy(
            src_ref=src, dst_ref=dst, send_sem=send, recv_sem=recv,
            device_id=device, device_id_type=MESH,
        )

    barrier = pltpu.get_barrier_semaphore()
    pl.semaphore_signal(barrier, inc=1, device_id=twin, device_id_type=MESH)
    for o in range(1, GROUP):
        p = lax.rem(flat + o, GROUP)
        pl.semaphore_signal(barrier, inc=1, device_id=on_plane(p), device_id_type=MESH)
    for o in range(1, 2 * Z):
        p = lax.rem(zz + o, 2 * Z)
        pl.semaphore_signal(barrier, inc=1, device_id=on_z(p), device_id_type=MESH)

    size = GROUP * PIECE
    r = lax.broadcasted_iota(jnp.int32, (size, size), 0)
    c = lax.broadcasted_iota(jnp.int32, (size, size), 1)
    home = ((r >> 3) & 3) * 64 + ((r >> 1) & 1) * 32 + ((r >> 2) & 1) * 16
    home = home + (r >> 7) * 8 + ((r >> 6) & 1) * 4 + (r & 1) * 2 + ((r >> 5) & 1)
    turn = (c == home).astype(jnp.bfloat16)
    slots = times(turn, back_ref[...].reshape(size, HALF), ((1,), (0,))).astype(jnp.bfloat16)

    def slot_rows(t, i):
        k = (t * 2 + i) * SLOTS
        return jnp.concatenate(
            [slots[h * 4 * SLOTS + k : h * 4 * SLOTS + k + SLOTS] for h in range(2)], axis=1
        )

    keys = keys_ref[...]
    weights, sums = [], None
    for i in range(2):
        slot_out, slot_dx = slot_rows(0, i), slot_rows(1, i)
        both = times(jnp.concatenate([keys, slot_dx], axis=0), tokens_ref[i], ((1,), (1,)))
        logits, disp_grad = both[:SLOTS], both[SLOTS:]
        dispatch, combine = soft(logits, 1), soft(logits, 0)
        comb_grad = times(slot_out, grad_ref[i], ((1,), (1,)))
        inner = jnp.sum(combine * comb_grad, axis=0, keepdims=True)
        comb_logit = combine * (comb_grad - inner)
        inner = jnp.sum(dispatch * disp_grad, axis=1, keepdims=True)
        disp_logit = dispatch * (disp_grad - inner)
        logit_grad = (comb_logit + disp_logit).astype(jnp.bfloat16)
        term = times(logit_grad, tokens_ref[i], ((1,), (0,)))
        sums = term if sums is None else sums + term
        weights.append(
            (
                jnp.concatenate([dispatch.astype(jnp.bfloat16), logit_grad], axis=0),
                jnp.concatenate([slot_dx, keys], axis=0),
            )
        )

    def token_grads(i):
        a, b = weights[i]
        dx_ref[i] = times(a, b, ((0,), (0,))).astype(jnp.bfloat16)

    for h in range(2):
        terms[h] = sums[h * SLOTS // 2 : (h + 1) * SLOTS // 2]
    pl.semaphore_wait(barrier, 1 + GROUP - 1 + 2 * Z - 1)
    to_twin = remote(terms.at[1 - core], other, send_c.at[0], recv_c.at[0], twin)
    to_twin.start()
    token_grads(0)
    to_twin.wait_recv()
    mine = terms[core] + other[...]
    for k in range(TILES):
        chunks[k] = mine[:, k * 128 : (k + 1) * 128]

    def to_owner(o):
        p = lax.rem(flat + o, GROUP)
        return remote(chunks.at[p], landed.at[o], send_a.at[o], recv_a.at[o], on_plane(p))

    def from_owner(o):
        p = lax.rem(flat + o, GROUP)
        return remote(total, done.at[flat], send_d.at[o], recv_d.at[o], on_plane(p))

    def across_z(o):
        p = lax.rem(zz + o, 2 * Z)
        return remote(part, parts_z.at[zz], send_z.at[o], recv_z.at[o], on_z(p))

    owner = flat < TILES
    for o in range(1, GROUP):

        @pl.when(lax.rem(flat + o, GROUP) < TILES)
        def _():
            to_owner(o).start()

    token_grads(1)

    @pl.when(owner)
    def _():
        acc = chunks[flat]
        for o in range(1, GROUP):
            to_owner(o).wait_recv()
            acc = acc + landed[o]
        part[...] = acc
        for o in range(1, 2 * Z):
            across_z(o).start()
        parts_z[zz] = acc
        for o in range(1, 2 * Z):
            across_z(o).wait_recv()
        acc = parts_z[0]
        for k in range(1, 2 * Z):
            acc = acc + parts_z[k]
        total[...] = acc
        for o in range(1, GROUP):
            from_owner(o).start()
        done[flat] = acc

    for o in range(1, GROUP):

        @pl.when(lax.rem(flat - o + GROUP, GROUP) < TILES)
        def _():
            from_owner(o).wait_recv()

    back_to_twin = remote(done.at[pl.ds(0, TILES)], done_other, send_c.at[1], recv_c.at[1], twin)
    back_to_twin.start()
    first = pl.ds(pl.multiple_of(core * (SLOTS // 2), SLOTS // 2), SLOTS // 2)
    second = pl.ds(pl.multiple_of((1 - core) * (SLOTS // 2), SLOTS // 2), SLOTS // 2)
    for k in range(TILES):
        keys_out_ref[first, k * 128 : (k + 1) * 128] = done[k]
    back_to_twin.wait_recv()
    for k in range(TILES):
        keys_out_ref[second, k * 128 : (k + 1) * 128] = done_other[k]

    to_twin.wait_send()
    back_to_twin.wait_send()
    for o in range(1, GROUP):

        @pl.when(lax.rem(flat + o, GROUP) < TILES)
        def _():
            to_owner(o).wait_send()

    @pl.when(owner)
    def _():
        for o in range(1, GROUP):
            from_owner(o).wait_send()
        for o in range(1, 2 * Z):
            across_z(o).wait_send()


def combine_gradients(tokens, grad_out, keys_turned, back):
    f32 = jnp.float32
    dma = pltpu.SemaphoreType.DMA
    vmem = pl.BlockSpec(memory_space=pltpu.VMEM)
    tile = (SLOTS // 2, 128)
    return pl.pallas_call(
        combine_kernel,
        out_shape=(
            jax.ShapeDtypeStruct(tokens.shape, jnp.bfloat16),
            jax.ShapeDtypeStruct(keys_turned.shape, f32),
        ),
        in_specs=[vmem] * 4,
        out_specs=(vmem,) * 2,
        scratch_shapes=[
            pltpu.VMEM((2, SLOTS // 2, D), f32),
            pltpu.VMEM((SLOTS // 2, D), f32),
            pltpu.VMEM((GROUP,) + tile, f32),
            pltpu.VMEM((GROUP,) + tile, f32),
            pltpu.VMEM(tile, f32),
            pltpu.VMEM((2 * Z,) + tile, f32),
            pltpu.VMEM(tile, f32),
            pltpu.VMEM((GROUP,) + tile, f32),
            pltpu.VMEM((TILES,) + tile, f32),
            dma((2,)), dma((2,)),
            dma((GROUP,)), dma((GROUP,)),
            dma((2 * Z,)), dma((2 * Z,)),
            dma((GROUP,)), dma((GROUP,)),
        ],
        compiler_params=pltpu.CompilerParams(
            collective_id=1, has_side_effects=True, vmem_limit_bytes=48 * 1024 * 1024
        ),
        name="combine",
    )(tokens, grad_out, keys_turned, back)


def exchange_kernel(
    tokens_ref, grad_ref, keys_ref, w_in_hbm, w_out_hbm,
    back_ref, grad_in_ref, grad_out_ref,
    w_in_ref, w_out_ref, pieces_ref, landed, own, rows, part, hid, pre, from_left, from_right, sum_left, sum_right, sum_z, ready,
    send_x, recv_x, send_b, recv_b, send_z, recv_z, send_s, recv_s,
    send_y, recv_y, send_h, recv_h, send_f, recv_f, send_p, recv_p, fetched,
):
    row, col = lax.axis_index("dp"), lax.axis_index("expert")
    yy = lax.rem(row, Y)
    zz = lax.rem(col // 2, 2) * Z + row // Y
    side = (col // 4) * 2 + lax.rem(col, 2)

    def on_side(o):
        p = lax.rem(side + o, SIDE)
        return p, (row, (p // 2) * 4 + lax.rem(col // 2, 2) * 2 + lax.rem(p, 2))

    def on_z(p):
        return (lax.rem(p, Z) * Y + yy, (col // 4) * 4 + (p // Z) * 2 + lax.rem(col, 2))

    def on_y(o):
        return ((row // Y) * Y + lax.rem(yy + o + Y, Y), col)

    right, left = on_y(1), on_y(-1)

    def remote(src, dst, send, recv, device):
        return pltpu.make_async_remote_copy(
            src_ref=src, dst_ref=dst, send_sem=send, recv_sem=recv,
            device_id=device, device_id_type=MESH,
        )

    barrier = pltpu.get_barrier_semaphore()
    for o in range(1, SIDE):
        pl.semaphore_signal(barrier, inc=1, device_id=on_side(o)[1], device_id_type=MESH)
        pl.semaphore_signal(
            barrier, inc=1, device_id=on_z(lax.rem(zz + o, 2 * Z)), device_id_type=MESH
        )
    pl.semaphore_signal(barrier, inc=1, device_id=right, device_id_type=MESH)
    pl.semaphore_signal(barrier, inc=1, device_id=left, device_id_type=MESH)
    w_in_copy = pltpu.make_async_copy(w_in_hbm, w_in_ref, fetched.at[0])
    w_out_copy = pltpu.make_async_copy(w_out_hbm, w_out_ref, fetched.at[1])
    w_in_copy.start()
    w_out_copy.start()

    size = GROUP * PIECE
    r = lax.broadcasted_iota(jnp.int32, (size, size), 0)
    c = lax.broadcasted_iota(jnp.int32, (size, size), 1)
    home = ((r >> 3) & 1) * 128 + ((r >> 2) & 1) * 64 + (r & 1) * 32
    home = home + (r >> 6) * 8 + ((r >> 4) & 1) * 4 + ((r >> 5) & 1) * 2 + ((r >> 1) & 1)
    order = (c == home).astype(jnp.bfloat16)
    slots = [[None, None], [None, None]]
    for i in range(2):
        logits = times(keys_ref[...], tokens_ref[i], ((1,), (1,)))
        dispatch, combine = soft(logits, 1), soft(logits, 0)
        for t, (share, x) in enumerate(((dispatch, tokens_ref), (combine, grad_ref))):
            seen = times(share.astype(jnp.bfloat16), x[i], ((1,), (0,)))
            slots[t][i] = seen.astype(jnp.bfloat16)
    stack = jnp.concatenate(
        [
            slots[t][i][:, h * HALF : (h + 1) * HALF]
            for h in range(2)
            for t in range(2)
            for i in range(2)
        ],
        axis=0,
    )
    pieces = times(order, stack, ((1,), (0,))).astype(jnp.bfloat16)
    pieces_ref[...] = pieces.reshape(SIDE, 2, PIECE, HALF)
    pl.semaphore_wait(barrier, 2 * (SIDE - 1) + 2)

    def piece_out(o):
        p, there = on_side(o)
        return remote(pieces_ref.at[p], landed.at[side], send_x.at[o], recv_x.at[o], there)

    for o in range(1, SIDE):
        piece_out(o).start()
    landed[side] = pieces_ref[side]

    size = SIDE * PIECE
    r = lax.broadcasted_iota(jnp.int32, (size, size), 0)
    c = lax.broadcasted_iota(jnp.int32, (size, size), 1)
    turn = (c == ((r >> 1) & 7) * 16 + (r >> 4) * 2 + (r & 1)).astype(jnp.bfloat16)

    def turned(x):
        return jnp.dot(turn, x, preferred_element_type=jnp.float32).astype(jnp.bfloat16)

    parts_of_piece = [(h, t, s) for h in range(2) for t in range(2) for s in range(2)]
    for o in range(1, SIDE):
        piece_out(o).wait_recv()
    for g in range(2):
        block = turned(landed[:, g].reshape(size, HALF))
        for k, (h, t, s) in enumerate(parts_of_piece):
            own[g, t, s, :, h * HALF : (h + 1) * HALF] = block[k * SEEN : (k + 1) * SEEN]

    def place(q):
        return lax.rem(zz - AWAY[q] + 2 * Z, 2 * Z)

    def along_z(q):
        p = lax.rem(zz + AWAY[q], 2 * Z)
        return remote(own.at[p // Z], rows.at[zz, yy], send_z.at[q], recv_z.at[q], on_z(p))

    def along_y(q, d):
        mine = rows.at[place(q), yy]
        return remote(mine, mine, send_y.at[q, d], recv_y.at[q, d], left if d else right)

    def onward(q, d):
        ours = rows.at[place(q), lax.rem(yy + (1 if d else Y - 1), Y), d]
        return remote(ours, ours, send_h.at[q, d], recv_h.at[q, d], left if d else right)

    def experts(q):
        p = place(q)
        for s in range(2):
            x = rows[p, :, 0, s].reshape(Y * SEEN, D)
            g = rows[p, :, 1, s].reshape(Y * SEEN, D)
            pre_act = times(x, w_in_ref[s], ((1,), (1,)))
            act_grad = times(g, w_out_ref[s], ((1,), (1,)))
            cdf = 0.5 * (1.0 + lax.erf(pre_act * INV_ROOT2))
            hidden = (pre_act * cdf).astype(jnp.bfloat16)
            slope = cdf + pre_act * jnp.exp(-0.5 * pre_act * pre_act) * INV_ROOT_TWO_PI
            pre_grad = (act_grad * slope).astype(jnp.bfloat16)
            hid[s, p] = hidden
            pre[s, p] = pre_grad
            out = times(hidden, w_out_ref[s], ((1,), (0,)))
            part[p, :, 0, s] = out.astype(jnp.bfloat16).reshape(Y, SEEN, D)
            back = times(pre_grad, w_in_ref[s], ((1,), (0,)))
            part[p, :, 1, s] = back.astype(jnp.bfloat16).reshape(Y, SEEN, D)

    def far(q, d):
        ours = part.at[place(q), lax.rem(yy + 2, Y), d]
        land = (from_right if d else from_left).at[q]
        return remote(ours, land, send_f.at[q, d], recv_f.at[q, d], left if d else right)

    def near(q, d):
        ours = part.at[place(q), lax.rem(yy + (Y - 1 if d else 1), Y)]
        land = (sum_right if d else sum_left).at[q]
        return remote(ours, land, send_p.at[q, d], recv_p.at[q, d], left if d else right)

    def along_z_back(q):
        p = place(q)
        return remote(part.at[p, yy], sum_z.at[zz], send_s.at[q], recv_s.at[q], on_z(p))

    def begin(q):
        for d in range(2):
            far(q, d).start()

    def pass_on(q):
        for d in range(2):
            far(q, d).wait_recv()
            ours = part.at[place(q), lax.rem(yy + (Y - 1 if d else 1), Y), d]
            other = (from_right if d else from_left)[q].astype(jnp.float32)
            ours[...] = (ours[...].astype(jnp.float32) + other).astype(jnp.bfloat16)
            near(q, d).start()

    def collect(q):
        for d in range(2):
            near(q, d).wait_recv()
        total = (
            part[place(q), yy].astype(jnp.float32)
            + sum_left[q].astype(jnp.float32)
            + sum_right[q].astype(jnp.float32)
        ).astype(jnp.bfloat16)
        if q == 0:
            sum_z[zz] = total
        else:
            part[place(q), yy] = total
            along_z_back(q).start()

    last = len(AWAY) - 1
    for q in range(1, 4):
        along_z(q).start()
    rows[zz, yy] = own[zz // Z]

    def fetch(q):
        if 1 <= q <= last:
            along_z(q).wait_recv()
            if q + 3 <= last:
                along_z(q + 3).start()
        if q <= last:
            for d in range(2):
                along_y(q, d).start()

    def spread(q):
        if q <= last:
            for d in range(2):
                along_y(q, d).wait_recv()
                onward(q, d).start()

    fetch(0)
    fetch(1)
    spread(0)
    w_in_copy.wait()
    w_out_copy.wait()
    for q in range(last + 1):
        fetch(q + 2)
        spread(q + 1)
        for d in range(2):
            onward(q, d).wait_recv()
        experts(q)
        if q >= 1:
            begin(q)
        if q >= 2:
            pass_on(q - 1)
        if q >= 3:
            collect(q - 2)
    begin(0)

    for s in range(2):
        p_all = pre[s].reshape(2 * Z * Y * SEEN, HID)
        h_all = hid[s].reshape(2 * Z * Y * SEEN, HID)
        for k in range(0, D, 256):
            x = rows[:, :, 0, s, :, k : k + 256].reshape(2 * Z * Y * SEEN, 256)
            g = rows[:, :, 1, s, :, k : k + 256].reshape(2 * Z * Y * SEEN, 256)
            grad_in_ref[s, :, k : k + 256] = times(p_all, x, ((0,), (0,))).astype(jnp.bfloat16)
            grad_out_ref[s, :, k : k + 256] = times(h_all, g, ((0,), (0,))).astype(jnp.bfloat16)
        if s == 0:
            pass_on(last)
            collect(last - 1)
            pass_on(0)
    collect(last)
    collect(0)

    for q in range(1, last + 1):
        along_z_back(q).wait_recv()
    for g in range(2):
        total = sum_z[g * Z].astype(jnp.float32)
        for k in range(1, Z):
            total = total + sum_z[g * Z + k].astype(jnp.float32)
        total = total.astype(jnp.bfloat16)
        stack = jnp.concatenate(
            [total[t, s, :, h * HALF : (h + 1) * HALF] for h, t, s in parts_of_piece], axis=0
        )
        ready[:, g] = turned(stack).reshape(SIDE, PIECE, HALF)

    def piece_back(o):
        p, there = on_side(o)
        return remote(ready.at[p], back_ref.at[side], send_b.at[o], recv_b.at[o], there)

    for o in range(1, SIDE):
        piece_back(o).start()
    back_ref[side] = ready[side]
    for o in range(1, SIDE):
        piece_back(o).wait_recv()

    for o in range(1, SIDE):
        piece_out(o).wait_send()
        piece_back(o).wait_send()
    for q in range(last + 1):
        if q > 0:
            along_z(q).wait_send()
            along_z_back(q).wait_send()
        for d in range(2):
            along_y(q, d).wait_send()
            onward(q, d).wait_send()
            far(q, d).wait_send()
            near(q, d).wait_send()


def expert_exchange(tokens, grad_out, keys_turned, w_in_turned, w_out):
    pieces = (SIDE, 2, PIECE, HALF)
    block = (2, 2, SEEN, D)
    slabs = 2 * Z
    bf16 = jnp.bfloat16
    dma = pltpu.SemaphoreType.DMA
    vmem = pl.BlockSpec(memory_space=pltpu.VMEM)
    return pl.pallas_call(
        exchange_kernel,
        out_shape=(
            jax.ShapeDtypeStruct(pieces, bf16),
            jax.ShapeDtypeStruct(w_out.shape, bf16),
            jax.ShapeDtypeStruct(w_out.shape, bf16),
        ),
        in_specs=[vmem] * 3 + [pl.BlockSpec(memory_space=pl.ANY)] * 2,
        out_specs=(vmem,) * 3,
        scratch_shapes=[
            pltpu.VMEM(w_out.shape, bf16),
            pltpu.VMEM(w_out.shape, bf16),
            pltpu.VMEM(pieces, bf16),
            pltpu.VMEM(pieces, bf16),
            pltpu.VMEM((2,) + block, bf16),
            pltpu.VMEM((slabs, Y) + block, bf16),
            pltpu.VMEM((slabs, Y) + block, bf16),
            pltpu.VMEM((2, slabs, Y * SEEN, HID), bf16),
            pltpu.VMEM((2, slabs, Y * SEEN, HID), bf16),
            pltpu.VMEM((slabs,) + block[1:], bf16),
            pltpu.VMEM((slabs,) + block[1:], bf16),
            pltpu.VMEM((slabs,) + block, bf16),
            pltpu.VMEM((slabs,) + block, bf16),
            pltpu.VMEM((slabs,) + block, bf16),
            pltpu.VMEM(pieces, bf16),
        ]
        + [dma((SIDE,))] * 8
        + [dma((slabs, 2))] * 8
        + [dma((2,))],
        compiler_params=pltpu.CompilerParams(
            collective_id=0, has_side_effects=True, vmem_limit_bytes=56 * 1024 * 1024
        ),
        name="experts",
    )(tokens, grad_out, keys_turned, w_in_turned, w_out)


def local(tokens, slot_keys, w_in, w_out, grad_out):
    keys_turned = slot_keys.T
    back, grad_w_in, grad_w_out = expert_exchange(
        tokens, grad_out, keys_turned, w_in.transpose(0, 2, 1), w_out
    )
    grad_tokens, grad_keys = combine_gradients(tokens, grad_out, keys_turned, back)
    return (grad_tokens, grad_keys.T, grad_w_in.transpose(0, 2, 1), grad_w_out)


def solution(mesh):
    return jax.shard_map(
        local,
        mesh=mesh,
        in_specs=(
            P(("dp", "expert"), None, None),
            P(),
            P("expert", None, "dp"),
            P("expert", "dp", None),
            P(("dp", "expert"), None, None),
        ),
        out_specs=(
            P(("dp", "expert"), None, None),
            P(),
            P("expert", None, "dp"),
            P("expert", "dp", None),
        ),
        check_vma=False,
    )
```

```python
import jax
import jax.numpy as jnp
from jax import lax
from jax.experimental import pallas as pl
from jax.experimental.pallas import tpu as pltpu
from jax.sharding import PartitionSpec as P

MESH = pl.DeviceIdType.MESH
GROUP = 16
Z, Y = 4, 4
D = 1280
HID = 320
HALF = D // 2
SLOTS = 32
TILES = D // 128
SIDE = 8
SEEN = 16
AWAY = (0, 1, 2, 6, 4, 3, 5, 7)
PIECE = 16

INV_ROOT2 = 0.7071067811865476
INV_ROOT_TWO_PI = 0.3989422804014327


def times(a, b, over):
    return lax.dot_general(a, b, (over, ((), ())), preferred_element_type=jnp.float32)


def soft(x, axis):
    e = jnp.exp(x - jnp.max(x, axis=axis, keepdims=True))
    return e / jnp.sum(e, axis=axis, keepdims=True)


def combine_kernel(
    tokens_ref, grad_ref, keys_ref, back_ref, dx_ref, keys_out_ref,
    terms, other, chunks, landed, part, parts_z, total, done, done_other,
    send_c, recv_c, send_a, recv_a, send_z, recv_z, send_d, recv_d,
):
    row, col = lax.axis_index("dp"), lax.axis_index("expert")
    xx, yy, core = col // 4, lax.rem(row, Y), lax.rem(col, 2)
    half_z = lax.rem(col // 2, 2)
    zz = half_z * Z + row // Y
    flat = xx * Y + yy

    def on_plane(p):
        return ((row // Y) * Y + lax.rem(p, Y), (p // Y) * 4 + half_z * 2 + core)

    def on_z(p):
        return (lax.rem(p, Z) * Y + yy, xx * 4 + (p // Z) * 2 + core)

    twin = (row, col - core + 1 - core)

    def remote(src, dst, send, recv, device):
        return pltpu.make_async_remote_copy(
            src_ref=src, dst_ref=dst, send_sem=send, recv_sem=recv,
            device_id=device, device_id_type=MESH,
        )

    barrier = pltpu.get_barrier_semaphore()
    pl.semaphore_signal(barrier, inc=1, device_id=twin, device_id_type=MESH)
    for o in range(1, GROUP):
        p = lax.rem(flat + o, GROUP)
        pl.semaphore_signal(barrier, inc=1, device_id=on_plane(p), device_id_type=MESH)
    for o in range(1, 2 * Z):
        p = lax.rem(zz + o, 2 * Z)
        pl.semaphore_signal(barrier, inc=1, device_id=on_z(p), device_id_type=MESH)

    size = GROUP * PIECE
    r = lax.broadcasted_iota(jnp.int32, (size, size), 0)
    c = lax.broadcasted_iota(jnp.int32, (size, size), 1)
    home = ((r >> 3) & 3) * 64 + ((r >> 1) & 1) * 32 + ((r >> 2) & 1) * 16
    home = home + (r >> 7) * 8 + ((r >> 6) & 1) * 4 + (r & 1) * 2 + ((r >> 5) & 1)
    turn = (c == home).astype(jnp.bfloat16)
    slots = times(turn, back_ref[...].reshape(size, HALF), ((1,), (0,))).astype(jnp.bfloat16)

    def slot_rows(t, i):
        k = (t * 2 + i) * SLOTS
        return jnp.concatenate(
            [slots[h * 4 * SLOTS + k : h * 4 * SLOTS + k + SLOTS] for h in range(2)], axis=1
        )

    keys = keys_ref[...]
    weights, sums = [], None
    for i in range(2):
        slot_out, slot_dx = slot_rows(0, i), slot_rows(1, i)
        both = times(jnp.concatenate([keys, slot_dx], axis=0), tokens_ref[i], ((1,), (1,)))
        logits, disp_grad = both[:SLOTS], both[SLOTS:]
        dispatch, combine = soft(logits, 1), soft(logits, 0)
        comb_grad = times(slot_out, grad_ref[i], ((1,), (1,)))
        inner = jnp.sum(combine * comb_grad, axis=0, keepdims=True)
        comb_logit = combine * (comb_grad - inner)
        inner = jnp.sum(dispatch * disp_grad, axis=1, keepdims=True)
        disp_logit = dispatch * (disp_grad - inner)
        logit_grad = (comb_logit + disp_logit).astype(jnp.bfloat16)
        term = times(logit_grad, tokens_ref[i], ((1,), (0,)))
        sums = term if sums is None else sums + term
        weights.append(
            (
                jnp.concatenate([dispatch.astype(jnp.bfloat16), logit_grad], axis=0),
                jnp.concatenate([slot_dx, keys], axis=0),
            )
        )

    def token_grads(i):
        a, b = weights[i]
        dx_ref[i] = times(a, b, ((0,), (0,))).astype(jnp.bfloat16)

    for h in range(2):
        terms[h] = sums[h * SLOTS // 2 : (h + 1) * SLOTS // 2]
    pl.semaphore_wait(barrier, 1 + GROUP - 1 + 2 * Z - 1)
    to_twin = remote(terms.at[1 - core], other, send_c.at[0], recv_c.at[0], twin)
    to_twin.start()
    token_grads(0)
    to_twin.wait_recv()
    mine = terms[core] + other[...]
    for k in range(TILES):
        chunks[k] = mine[:, k * 128 : (k + 1) * 128]

    def to_owner(o):
        p = lax.rem(flat + o, GROUP)
        return remote(chunks.at[p], landed.at[o], send_a.at[o], recv_a.at[o], on_plane(p))

    def from_owner(o):
        p = lax.rem(flat + o, GROUP)
        return remote(total, done.at[flat], send_d.at[o], recv_d.at[o], on_plane(p))

    def across_z(o):
        p = lax.rem(zz + o, 2 * Z)
        return remote(part, parts_z.at[zz], send_z.at[o], recv_z.at[o], on_z(p))

    owner = flat < TILES
    for o in range(1, GROUP):

        @pl.when(lax.rem(flat + o, GROUP) < TILES)
        def _():
            to_owner(o).start()

    token_grads(1)

    @pl.when(owner)
    def _():
        acc = chunks[flat]
        for o in range(1, GROUP):
            to_owner(o).wait_recv()
            acc = acc + landed[o]
        part[...] = acc
        for o in range(1, 2 * Z):
            across_z(o).start()
        parts_z[zz] = acc
        for o in range(1, 2 * Z):
            across_z(o).wait_recv()
        acc = parts_z[0]
        for k in range(1, 2 * Z):
            acc = acc + parts_z[k]
        total[...] = acc
        for o in range(1, GROUP):
            from_owner(o).start()
        done[flat] = acc

    for o in range(1, GROUP):

        @pl.when(lax.rem(flat - o + GROUP, GROUP) < TILES)
        def _():
            from_owner(o).wait_recv()

    back_to_twin = remote(done.at[pl.ds(0, TILES)], done_other, send_c.at[1], recv_c.at[1], twin)
    back_to_twin.start()
    first = pl.ds(pl.multiple_of(core * (SLOTS // 2), SLOTS // 2), SLOTS // 2)
    second = pl.ds(pl.multiple_of((1 - core) * (SLOTS // 2), SLOTS // 2), SLOTS // 2)
    for k in range(TILES):
        keys_out_ref[first, k * 128 : (k + 1) * 128] = done[k]
    back_to_twin.wait_recv()
    for k in range(TILES):
        keys_out_ref[second, k * 128 : (k + 1) * 128] = done_other[k]

    to_twin.wait_send()
    back_to_twin.wait_send()
    for o in range(1, GROUP):

        @pl.when(lax.rem(flat + o, GROUP) < TILES)
        def _():
            to_owner(o).wait_send()

    @pl.when(owner)
    def _():
        for o in range(1, GROUP):
            from_owner(o).wait_send()
        for o in range(1, 2 * Z):
            across_z(o).wait_send()


def combine_gradients(tokens, grad_out, keys_turned, back):
    f32 = jnp.float32
    dma = pltpu.SemaphoreType.DMA
    vmem = pl.BlockSpec(memory_space=pltpu.VMEM)
    tile = (SLOTS // 2, 128)
    return pl.pallas_call(
        combine_kernel,
        out_shape=(
            jax.ShapeDtypeStruct(tokens.shape, jnp.bfloat16),
            jax.ShapeDtypeStruct(keys_turned.shape, f32),
        ),
        in_specs=[vmem] * 4,
        out_specs=(vmem,) * 2,
        scratch_shapes=[
            pltpu.VMEM((2, SLOTS // 2, D), f32),
            pltpu.VMEM((SLOTS // 2, D), f32),
            pltpu.VMEM((GROUP,) + tile, f32),
            pltpu.VMEM((GROUP,) + tile, f32),
            pltpu.VMEM(tile, f32),
            pltpu.VMEM((2 * Z,) + tile, f32),
            pltpu.VMEM(tile, f32),
            pltpu.VMEM((GROUP,) + tile, f32),
            pltpu.VMEM((TILES,) + tile, f32),
            dma((2,)), dma((2,)),
            dma((GROUP,)), dma((GROUP,)),
            dma((2 * Z,)), dma((2 * Z,)),
            dma((GROUP,)), dma((GROUP,)),
        ],
        compiler_params=pltpu.CompilerParams(
            collective_id=1, has_side_effects=True, vmem_limit_bytes=48 * 1024 * 1024
        ),
        name="combine",
    )(tokens, grad_out, keys_turned, back)


def exchange_kernel(
    tokens_ref, grad_ref, keys_ref, w_in_hbm, w_out_hbm,
    back_ref, grad_in_hbm, grad_out_hbm,
    w_in_ref, w_out_ref, grad_in_ref, grad_out_ref, pieces_ref, landed, own, rows, part, hid, pre, from_left, from_right, sum_left, sum_right, sum_z, ready,
    send_x, recv_x, send_b, recv_b, send_z, recv_z, send_s, recv_s,
    send_y, recv_y, send_h, recv_h, send_f, recv_f, send_p, recv_p, fetched,
):
    row, col = lax.axis_index("dp"), lax.axis_index("expert")
    yy = lax.rem(row, Y)
    zz = lax.rem(col // 2, 2) * Z + row // Y
    side = (col // 4) * 2 + lax.rem(col, 2)

    def on_side(o):
        p = lax.rem(side + o, SIDE)
        return p, (row, (p // 2) * 4 + lax.rem(col // 2, 2) * 2 + lax.rem(p, 2))

    def on_z(p):
        return (lax.rem(p, Z) * Y + yy, (col // 4) * 4 + (p // Z) * 2 + lax.rem(col, 2))

    def on_y(o):
        return ((row // Y) * Y + lax.rem(yy + o + Y, Y), col)

    right, left = on_y(1), on_y(-1)

    def remote(src, dst, send, recv, device):
        return pltpu.make_async_remote_copy(
            src_ref=src, dst_ref=dst, send_sem=send, recv_sem=recv,
            device_id=device, device_id_type=MESH,
        )

    barrier = pltpu.get_barrier_semaphore()
    for o in range(1, SIDE):
        pl.semaphore_signal(barrier, inc=1, device_id=on_side(o)[1], device_id_type=MESH)
        pl.semaphore_signal(
            barrier, inc=1, device_id=on_z(lax.rem(zz + o, 2 * Z)), device_id_type=MESH
        )
    pl.semaphore_signal(barrier, inc=1, device_id=right, device_id_type=MESH)
    pl.semaphore_signal(barrier, inc=1, device_id=left, device_id_type=MESH)
    w_in_copy = pltpu.make_async_copy(w_in_hbm, w_in_ref, fetched.at[0])
    w_out_copy = pltpu.make_async_copy(w_out_hbm, w_out_ref, fetched.at[1])
    w_in_copy.start()
    w_out_copy.start()

    size = GROUP * PIECE
    r = lax.broadcasted_iota(jnp.int32, (size, size), 0)
    c = lax.broadcasted_iota(jnp.int32, (size, size), 1)
    home = ((r >> 3) & 1) * 128 + ((r >> 2) & 1) * 64 + (r & 1) * 32
    home = home + (r >> 6) * 8 + ((r >> 4) & 1) * 4 + ((r >> 5) & 1) * 2 + ((r >> 1) & 1)
    order = (c == home).astype(jnp.bfloat16)
    slots = [[None, None], [None, None]]
    for i in range(2):
        logits = times(keys_ref[...], tokens_ref[i], ((1,), (1,)))
        dispatch, combine = soft(logits, 1), soft(logits, 0)
        for t, (share, x) in enumerate(((dispatch, tokens_ref), (combine, grad_ref))):
            seen = times(share.astype(jnp.bfloat16), x[i], ((1,), (0,)))
            slots[t][i] = seen.astype(jnp.bfloat16)
    stack = jnp.concatenate(
        [
            slots[t][i][:, h * HALF : (h + 1) * HALF]
            for h in range(2)
            for t in range(2)
            for i in range(2)
        ],
        axis=0,
    )
    pieces = times(order, stack, ((1,), (0,))).astype(jnp.bfloat16)
    pieces_ref[...] = pieces.reshape(SIDE, 2, PIECE, HALF)
    pl.semaphore_wait(barrier, 2 * (SIDE - 1) + 2)

    def piece_out(o):
        p, there = on_side(o)
        return remote(pieces_ref.at[p], landed.at[side], send_x.at[o], recv_x.at[o], there)

    for o in range(1, SIDE):
        piece_out(o).start()
    landed[side] = pieces_ref[side]

    size = SIDE * PIECE
    r = lax.broadcasted_iota(jnp.int32, (size, size), 0)
    c = lax.broadcasted_iota(jnp.int32, (size, size), 1)
    turn = (c == ((r >> 1) & 7) * 16 + (r >> 4) * 2 + (r & 1)).astype(jnp.bfloat16)

    def turned(x):
        return jnp.dot(turn, x, preferred_element_type=jnp.float32).astype(jnp.bfloat16)

    parts_of_piece = [(h, t, s) for h in range(2) for t in range(2) for s in range(2)]
    for o in range(1, SIDE):
        piece_out(o).wait_recv()
    for g in range(2):
        block = turned(landed[:, g].reshape(size, HALF))
        for k, (h, t, s) in enumerate(parts_of_piece):
            own[g, t, s, :, h * HALF : (h + 1) * HALF] = block[k * SEEN : (k + 1) * SEEN]

    def place(q):
        return lax.rem(zz - AWAY[q] + 2 * Z, 2 * Z)

    def along_z(q):
        p = lax.rem(zz + AWAY[q], 2 * Z)
        return remote(own.at[p // Z], rows.at[zz, yy], send_z.at[q], recv_z.at[q], on_z(p))

    def along_y(q, d):
        mine = rows.at[place(q), yy]
        return remote(mine, mine, send_y.at[q, d], recv_y.at[q, d], left if d else right)

    def onward(q, d):
        ours = rows.at[place(q), lax.rem(yy + (1 if d else Y - 1), Y), d]
        return remote(ours, ours, send_h.at[q, d], recv_h.at[q, d], left if d else right)

    def experts(q):
        p = place(q)
        for s in range(2):
            x = rows[p, :, 0, s].reshape(Y * SEEN, D)
            g = rows[p, :, 1, s].reshape(Y * SEEN, D)
            pre_act = times(x, w_in_ref[s], ((1,), (1,)))
            act_grad = times(g, w_out_ref[s], ((1,), (1,)))
            cdf = 0.5 * (1.0 + lax.erf(pre_act * INV_ROOT2))
            hidden = (pre_act * cdf).astype(jnp.bfloat16)
            slope = cdf + pre_act * jnp.exp(-0.5 * pre_act * pre_act) * INV_ROOT_TWO_PI
            pre_grad = (act_grad * slope).astype(jnp.bfloat16)
            hid[s, p] = hidden
            pre[s, p] = pre_grad
            out = times(hidden, w_out_ref[s], ((1,), (0,)))
            part[p, :, 0, s] = out.astype(jnp.bfloat16).reshape(Y, SEEN, D)
            back = times(pre_grad, w_in_ref[s], ((1,), (0,)))
            part[p, :, 1, s] = back.astype(jnp.bfloat16).reshape(Y, SEEN, D)

    def far(q, d):
        ours = part.at[place(q), lax.rem(yy + 2, Y), d]
        land = (from_right if d else from_left).at[q]
        return remote(ours, land, send_f.at[q, d], recv_f.at[q, d], left if d else right)

    def near(q, d):
        ours = part.at[place(q), lax.rem(yy + (Y - 1 if d else 1), Y)]
        land = (sum_right if d else sum_left).at[q]
        return remote(ours, land, send_p.at[q, d], recv_p.at[q, d], left if d else right)

    def along_z_back(q):
        p = place(q)
        return remote(part.at[p, yy], sum_z.at[zz], send_s.at[q], recv_s.at[q], on_z(p))

    def begin(q):
        for d in range(2):
            far(q, d).start()

    def pass_on(q):
        for d in range(2):
            far(q, d).wait_recv()
            ours = part.at[place(q), lax.rem(yy + (Y - 1 if d else 1), Y), d]
            other = (from_right if d else from_left)[q].astype(jnp.float32)
            ours[...] = (ours[...].astype(jnp.float32) + other).astype(jnp.bfloat16)
            near(q, d).start()

    def collect(q):
        for d in range(2):
            near(q, d).wait_recv()
        total = (
            part[place(q), yy].astype(jnp.float32)
            + sum_left[q].astype(jnp.float32)
            + sum_right[q].astype(jnp.float32)
        ).astype(jnp.bfloat16)
        if q == 0:
            sum_z[zz] = total
        else:
            part[place(q), yy] = total
            along_z_back(q).start()

    last = len(AWAY) - 1
    for q in range(1, last + 1):
        along_z(q).start()
    rows[zz, yy] = own[zz // Z]

    def fetch(q):
        if 1 <= q <= last:
            along_z(q).wait_recv()
        if q <= last:
            for d in range(2):
                along_y(q, d).start()

    def spread(q):
        if q <= last:
            for d in range(2):
                along_y(q, d).wait_recv()
                onward(q, d).start()

    fetch(0)
    fetch(1)
    spread(0)
    w_in_copy.wait()
    w_out_copy.wait()
    for q in range(last + 1):
        fetch(q + 2)
        spread(q + 1)
        for d in range(2):
            onward(q, d).wait_recv()
        experts(q)
        if q >= 1:
            begin(q)
        if q >= 2:
            pass_on(q - 1)
        if q >= 3:
            collect(q - 2)

    def weight_copies(s):
        return [
            pltpu.make_async_copy(ours.at[s], out.at[s], fetched.at[2 + 2 * s + k])
            for k, (ours, out) in enumerate(((grad_in_ref, grad_in_hbm), (grad_out_ref, grad_out_hbm)))
        ]

    def weight_grads(s):
        p_all = pre[s].reshape(2 * Z * Y * SEEN, HID)
        h_all = hid[s].reshape(2 * Z * Y * SEEN, HID)
        for k in range(0, D, 256):
            x = rows[:, :, 0, s, :, k : k + 256].reshape(2 * Z * Y * SEEN, 256)
            g = rows[:, :, 1, s, :, k : k + 256].reshape(2 * Z * Y * SEEN, 256)
            grad_in_ref[s, :, k : k + 256] = times(p_all, x, ((0,), (0,))).astype(jnp.bfloat16)
            grad_out_ref[s, :, k : k + 256] = times(h_all, g, ((0,), (0,))).astype(jnp.bfloat16)
        for copy in weight_copies(s):
            copy.start()

    weight_grads(0)
    pass_on(last)
    begin(0)
    collect(last - 1)
    weight_grads(1)
    pass_on(0)
    collect(last)
    collect(0)

    for q in range(1, last + 1):
        along_z_back(q).wait_recv()
    for g in range(2):
        total = sum_z[g * Z].astype(jnp.float32)
        for k in range(1, Z):
            total = total + sum_z[g * Z + k].astype(jnp.float32)
        total = total.astype(jnp.bfloat16)
        stack = jnp.concatenate(
            [total[t, s, :, h * HALF : (h + 1) * HALF] for h, t, s in parts_of_piece], axis=0
        )
        ready[:, g] = turned(stack).reshape(SIDE, PIECE, HALF)

    def piece_back(o):
        p, there = on_side(o)
        return remote(ready.at[p], back_ref.at[side], send_b.at[o], recv_b.at[o], there)

    for o in range(1, SIDE):
        piece_back(o).start()
    back_ref[side] = ready[side]
    for o in range(1, SIDE):
        piece_back(o).wait_recv()

    for s in range(2):
        for copy in weight_copies(s):
            copy.wait()
    for o in range(1, SIDE):
        piece_out(o).wait_send()
        piece_back(o).wait_send()
    for q in range(last + 1):
        if q > 0:
            along_z(q).wait_send()
            along_z_back(q).wait_send()
        for d in range(2):
            along_y(q, d).wait_send()
            onward(q, d).wait_send()
            far(q, d).wait_send()
            near(q, d).wait_send()


def expert_exchange(tokens, grad_out, keys_turned, w_in_turned, w_out):
    pieces = (SIDE, 2, PIECE, HALF)
    block = (2, 2, SEEN, D)
    slabs = 2 * Z
    bf16 = jnp.bfloat16
    dma = pltpu.SemaphoreType.DMA
    vmem = pl.BlockSpec(memory_space=pltpu.VMEM)
    return pl.pallas_call(
        exchange_kernel,
        out_shape=(
            jax.ShapeDtypeStruct(pieces, bf16),
            jax.ShapeDtypeStruct(w_out.shape, bf16),
            jax.ShapeDtypeStruct(w_out.shape, bf16),
        ),
        in_specs=[vmem] * 3 + [pl.BlockSpec(memory_space=pl.ANY)] * 2,
        out_specs=(vmem,) + (pl.BlockSpec(memory_space=pl.ANY),) * 2,
        scratch_shapes=[
            pltpu.VMEM(w_out.shape, bf16),
            pltpu.VMEM(w_out.shape, bf16),
            pltpu.VMEM(w_out.shape, bf16),
            pltpu.VMEM(w_out.shape, bf16),
            pltpu.VMEM(pieces, bf16),
            pltpu.VMEM(pieces, bf16),
            pltpu.VMEM((2,) + block, bf16),
            pltpu.VMEM((slabs, Y) + block, bf16),
            pltpu.VMEM((slabs, Y) + block, bf16),
            pltpu.VMEM((2, slabs, Y * SEEN, HID), bf16),
            pltpu.VMEM((2, slabs, Y * SEEN, HID), bf16),
            pltpu.VMEM((slabs,) + block[1:], bf16),
            pltpu.VMEM((slabs,) + block[1:], bf16),
            pltpu.VMEM((slabs,) + block, bf16),
            pltpu.VMEM((slabs,) + block, bf16),
            pltpu.VMEM((slabs,) + block, bf16),
            pltpu.VMEM(pieces, bf16),
        ]
        + [dma((SIDE,))] * 8
        + [dma((slabs, 2))] * 8
        + [dma((6,))],
        compiler_params=pltpu.CompilerParams(
            collective_id=0, has_side_effects=True, vmem_limit_bytes=56 * 1024 * 1024
        ),
        name="experts",
    )(tokens, grad_out, keys_turned, w_in_turned, w_out)


def settle_kernel(*refs):
    count = (len(refs) - 1) // 2
    done = refs[-1]
    copies = [
        pltpu.make_async_copy(src.at[k], dst.at[k], done.at[j, k])
        for j, (src, dst) in enumerate(zip(refs[:count], refs[count : 2 * count]))
        for k in range(2)
    ]
    for copy in copies:
        copy.start()
    for copy in copies:
        copy.wait()


def settled(*arrays):
    anywhere = pl.BlockSpec(memory_space=pl.ANY)
    return pl.pallas_call(
        settle_kernel,
        out_shape=tuple(jax.ShapeDtypeStruct(a.shape, a.dtype) for a in arrays),
        in_specs=[pl.BlockSpec(memory_space=pltpu.VMEM)] * len(arrays),
        out_specs=(anywhere,) * len(arrays),
        scratch_shapes=[pltpu.SemaphoreType.DMA((len(arrays), 2))],
        compiler_params=pltpu.CompilerParams(vmem_limit_bytes=16 * 1024 * 1024),
        name="settle",
    )(*arrays)


def local(tokens, slot_keys, w_in, w_out, grad_out):
    keys_turned = slot_keys.T
    back, grad_w_in, grad_w_out = expert_exchange(
        tokens, grad_out, keys_turned, w_in.transpose(0, 2, 1), w_out
    )
    grad_tokens, grad_keys = combine_gradients(tokens, grad_out, keys_turned, back)
    grad_tokens, grad_keys, grad_w_in, grad_w_out = settled(
        grad_tokens, grad_keys.reshape(2, SLOTS // 2, D), grad_w_in, grad_w_out
    )
    grad_keys = grad_keys.reshape(SLOTS, D)
    return (grad_tokens, grad_keys.T, grad_w_in.transpose(0, 2, 1), grad_w_out)


def solution(mesh):
    return jax.shard_map(
        local,
        mesh=mesh,
        in_specs=(
            P(("dp", "expert"), None, None),
            P(),
            P("expert", None, "dp"),
            P("expert", "dp", None),
            P(("dp", "expert"), None, None),
        ),
        out_specs=(
            P(("dp", "expert"), None, None),
            P(),
            P("expert", None, "dp"),
            P("expert", "dp", None),
        ),
        check_vma=False,
    )
```
